32 devices in a mesh: ka: 16 (over z, x, core), ga: 2 (over y).
Axes of the slice: x: 2, y: 2, z: 4, core: 2. Of those that a mesh axis runs over, the one named last changes fastest.
Arguments:
- row_orbitals: bfloat16 [4, 32, 4096], replicated, may hold values from -6 to 6
- orbitals: bfloat16 [64, 32, 4096], P('ka'), may hold values from -6 to 6
- screening: bfloat16 [1152, 304, 304], P('ka', None, 'ga'), may hold values from -0.3125 to 0.3125
- pair_blocks: int32 [64, 4], replicated, may hold values from 0 to 1151, as said below
- row_vectors: bfloat16 [4, 4, 256], replicated, may hold values from -6 to 6
- vectors: bfloat16 [4, 64, 256], P(None, 'ka'), may hold values from -6 to 6
Outputs:
- row_image: float32 [4, 4, 256], replicated
- column_image: float32 [4, 64, 256], P(None, 'ka')
The draws below stay inside these ranges and needn't reach their ends.
Inputs may be any that keep to these rules, and one draw needn't show every extreme that they name: `pair_blocks`: block q lies on index q // 72 of ka. In each aligned block of 4 rows (all 4 columns), at most 2 entries share one value of q // 72, and exactly 2 do for some value.
All inputs are finite; a program needn't handle non-finite values.
Results may differ from the reference program's by a relative error of at most 0.0081.
Values may be sent and summed in bfloat16 or wider, within the bound.
No kernel may reach another device: no remote copies, remote signals or barrier semaphores. Data moves between devices by JAX's collectives and lax.ppermute only.
A program may use at most 128 MiB of HBM per device.

```python
import math
import jax
import jax.numpy as jnp
from jax import lax

NV = 16
NC = 16
NB = 32
NG = 304
R = 4096
NVEC = 4
KR = 4
KPD = 4
QDEV = 72
CAP = 2
KP = 64
QN = 1152
N_KA = 16


def draw_pair_blocks(key, part):
    key = jax.random.fold_in(key, 11)
    order_key, place_key, block_key = jax.random.split(key, 3)
    pair_count = KPD * KR
    owners = jax.vmap(lambda sub_key: jax.random.permutation(sub_key, N_KA))(jax.random.split(order_key, N_KA))
    chosen = owners[:, jnp.arange(pair_count) // CAP]
    places = jax.vmap(lambda sub_key: jax.random.permutation(sub_key, pair_count))(jax.random.split(place_key, N_KA))
    chosen = jnp.take_along_axis(chosen, places, axis=1)
    local_block = jax.random.randint(block_key, (N_KA, pair_count), 0, QDEV)
    return (chosen * QDEV + local_block).astype(jnp.int32).reshape(N_KA * KPD, KR)


def level_of(key, shape, shards, low, largest):
    loudness = 1.0
    for axis_at, blocks in shards:
        draws = jax.random.uniform(jax.random.fold_in(jax.random.fold_in(key, 6), axis_at), (blocks,), jnp.float32, low / len(shards), largest / len(shards))
        loudness = loudness * jnp.repeat(jnp.exp(draws), shape[axis_at] // blocks).reshape((-1,) + (1,) * (len(shape) - 1 - axis_at))
    return loudness


def gaussian(own_key, dims, width, most, shards=(), dtype=jnp.bfloat16):
    entries = jax.random.normal(own_key, dims, jnp.float32) * width
    if len(shards) > 0:
        entries = level_of(own_key, dims, shards, -0.22, 0.18) * entries
    return jnp.clip(entries, min=-most, max=most).astype(dtype)


def setup_inputs(seed: int = 0) -> dict:
    arg_keys = jax.random.split(jax.random.key(seed), 7)
    row_orbitals = gaussian(arg_keys[0], (KR, NB, R), 1.0, 6.0)
    orbitals = gaussian(arg_keys[1], (KP, NB, R), 1.0, 6.0, ((0, 16),))
    screening = gaussian(arg_keys[2], (QN, NG, NG), NG ** -0.5, 0.3125, ((0, 16), (2, 2)))
    pair_blocks = draw_pair_blocks(jax.random.fold_in(arg_keys[6], 71), 0)
    row_vectors = gaussian(arg_keys[4], (NVEC, KR, NV * NC), 1.0, 6.0)
    vectors = gaussian(arg_keys[5], (NVEC, KP, NV * NC), 1.0, 6.0, ((1, 16),))
    return dict(row_orbitals=row_orbitals, orbitals=orbitals, screening=screening, pair_blocks=pair_blocks, row_vectors=row_vectors, vectors=vectors)


def plane_rows(first, count, grid):
    wave = (first + lax.iota(jnp.int32, count))[:, None]
    point = lax.iota(jnp.int32, grid)[None, :]
    phase = (wave * point % grid).astype(jnp.float32) * (2.0 * math.pi / grid)
    return math.sqrt(2.0 / grid) * jnp.cos(phase)

def densities_one(plane, row_bands, orbitals, lower, upper):
    grid = orbitals.shape[2]
    band_count = upper - lower
    weighted = (plane[:, None, :] * row_bands[lower:upper].astype(jnp.float32)[None]).astype(jnp.bfloat16)
    product = lax.dot_general(weighted.reshape(-1, grid), orbitals[:, lower:upper].reshape(-1, grid), (((1,), (1,)), ((), ())), preferred_element_type=jnp.float32)
    product = product.reshape(plane.shape[0], band_count, orbitals.shape[0], band_count)
    return product.transpose(2, 0, 1, 3).astype(jnp.bfloat16)

def rounded(values):
    return lax.optimization_barrier(values.astype(jnp.bfloat16)).astype(jnp.float32)

def reference(row_orbitals, orbitals, screening, pair_blocks, row_vectors, vectors):
    plane = plane_rows(0, NG, R)
    point_count = orbitals.shape[0]
    vec_all = vectors.astype(jnp.float32).reshape(NVEC, point_count, NV, NC)
    vec_row = row_vectors.astype(jnp.float32).reshape(NVEC, KR, NV, NC)
    row_parts = []
    column_total = jnp.zeros((NVEC, point_count, NV, NC), jnp.float32)
    for row_index in range(KR):
        cond = densities_one(plane, row_orbitals[row_index], orbitals, NV, NV + NC).astype(jnp.float32)
        vale = densities_one(plane, row_orbitals[row_index], orbitals, 0, NV).astype(jnp.float32)
        chosen = screening[pair_blocks[:, row_index]].astype(jnp.float32)
        screened = jnp.einsum('bgh,bhx->bgx', chosen, vale.reshape(point_count, NG, NV * NV))
        screened = rounded(screened).reshape(point_count, NG, NV, NV)
        first = rounded(jnp.einsum('bgcd,nbvd->bgcvn', cond, vec_all))
        row_parts.append(jnp.einsum('bgvw,bgcwn->nvc', screened, first))
        second = rounded(jnp.einsum('bgcd,nvc->bgdvn', cond, vec_row[:, row_index]))
        column_total = column_total + jnp.einsum('bgvw,bgdvn->nbwd', screened, second)
    row_scale = float(NG * NV * NC * point_count) ** (-0.5)
    column_scale = float(NG * NV * NC * KR) ** (-0.5)
    row_image = jnp.stack(row_parts, axis=1).reshape(NVEC, KR, NV * NC) * row_scale
    column_image = column_total.reshape(NVEC, point_count, NV * NC) * column_scale
    return (row_image, column_image)
```

```python
import math

import jax
import jax.numpy as jnp
from jax import lax
from jax.experimental import pallas as pl
from jax.experimental.pallas import tpu as pltpu
from jax.sharding import PartitionSpec as P

NV = 16
NC = 16
CAP = 2
MAIN = 256
HALF = 64
WIDE = CAP * MAIN + 2 * HALF


def plane_columns(first, count, grid, width):
    column = lax.broadcasted_iota(jnp.int32, (grid, width), 1)
    point = lax.broadcasted_iota(jnp.int32, (grid, width), 0)
    phase = ((first + column) * point % grid).astype(jnp.float32) * (2.0 * math.pi / grid)
    wave = math.sqrt(2.0 / grid) * jnp.cos(phase)
    return jnp.where(column < count, wave, 0.0).astype(jnp.bfloat16)


def gather_blocks(table, me, blocks, rows_per):
    n_dest = table.shape[0] // rows_per
    block_local, depth, waves = blocks.shape
    rest = waves - MAIN

    def kernel(table_ref, me_ref, blocks_ref, out_ref, held, packed, count, in_sem, out_sem):
        base = me_ref[0] * block_local

        def start(d, carry):
            taken = jnp.int32(0)
            for p in range(rows_per):
                local = table_ref[d * rows_per + p] - base
                hit = (local >= 0) & (local < block_local) & (taken < CAP)

                @pl.when(hit)
                def _():
                    at = d * CAP + taken
                    pltpu.make_async_copy(blocks_ref.at[local], held.at[at], in_sem.at[at]).start()

                taken = taken + hit.astype(jnp.int32)
            count[d] = taken
            return carry

        lax.fori_loop(0, n_dest, start, 0)

        def pack(d, carry):
            for s in range(CAP):

                @pl.when(count[d] > s)
                def _():
                    at = d * CAP + s
                    pltpu.make_async_copy(blocks_ref.at[0], held.at[at], in_sem.at[at]).wait()
                    packed[d, :, s * MAIN : (s + 1) * MAIN] = held[at, :, :MAIN]
                    low = CAP * MAIN + s * HALF
                    packed[d, :, low : low + rest] = held[at, :, MAIN:]

            pltpu.make_async_copy(packed.at[d], out_ref.at[d], out_sem.at[d]).start()
            return carry

        lax.fori_loop(0, n_dest, pack, 0)

        def finish(d, carry):
            pltpu.make_async_copy(packed.at[d], out_ref.at[d], out_sem.at[d]).wait()
            return carry

        lax.fori_loop(0, n_dest, finish, 0)

    return pl.pallas_call(
        kernel,
        out_shape=jax.ShapeDtypeStruct((n_dest, depth, WIDE), jnp.bfloat16),
        in_specs=[
            pl.BlockSpec(memory_space=pltpu.SMEM),
            pl.BlockSpec(memory_space=pltpu.SMEM),
            pl.BlockSpec(memory_space=pl.ANY),
        ],
        out_specs=pl.BlockSpec(memory_space=pl.ANY),
        scratch_shapes=[
            pltpu.VMEM((n_dest * CAP, depth, waves), jnp.bfloat16),
            pltpu.VMEM((n_dest, depth, WIDE), jnp.bfloat16),
            pltpu.SMEM((n_dest,), jnp.int32),
            pltpu.SemaphoreType.DMA((n_dest * CAP,)),
            pltpu.SemaphoreType.DMA((n_dest,)),
        ],
        compiler_params=pltpu.CompilerParams(vmem_limit_bytes=40 << 20),
        name="gather_blocks",
    )(table, me, blocks)


def densities(row_orbitals, orbitals, plane_vale, plane_cond):
    row_count, bands, grid = row_orbitals.shape
    point_local = orbitals.shape[0]
    depth = plane_vale.shape[1]
    width = plane_cond.shape[1]
    pairs = NV * NV

    def kernel(row_ref, orb_ref, vplane_ref, cplane_ref, vale_ref, cond_ref, fv, fc):
        def products(t, carry):
            lanes = pl.ds(pl.multiple_of(t * 128, 128), 128)
            for low, out in ((0, fv), (NV, fc)):
                ket = orb_ref[0, low : low + 16, lanes]
                for c in range(16):
                    bra = row_ref[0, low + c : low + c + 1, lanes]
                    out[c * 16 : (c + 1) * 16, lanes] = (bra * ket).astype(jnp.bfloat16)
            return carry

        lax.fori_loop(0, grid // 128, products, 0)
        vale_ref[0, 0] = jnp.dot(
            fv[...], vplane_ref[...], preferred_element_type=jnp.float32
        ).astype(jnp.bfloat16)
        cond_ref[0, 0] = jnp.dot(
            fc[...], cplane_ref[...], preferred_element_type=jnp.float32
        ).astype(jnp.bfloat16)

    return pl.pallas_call(
        kernel,
        grid=(point_local, row_count),
        out_shape=(
            jax.ShapeDtypeStruct((point_local, row_count, pairs, depth), jnp.bfloat16),
            jax.ShapeDtypeStruct((point_local, row_count, pairs, width), jnp.bfloat16),
        ),
        in_specs=[
            pl.BlockSpec((1, bands, grid), lambda b, a: (a, 0, 0)),
            pl.BlockSpec((1, bands, grid), lambda b, a: (b, 0, 0)),
            pl.BlockSpec((grid, depth), lambda b, a: (0, 0)),
            pl.BlockSpec((grid, width), lambda b, a: (0, 0)),
        ],
        out_specs=(
            pl.BlockSpec((1, 1, pairs, depth), lambda b, a: (b, a, 0, 0)),
            pl.BlockSpec((1, 1, pairs, width), lambda b, a: (b, a, 0, 0)),
        ),
        scratch_shapes=[
            pltpu.VMEM((pairs, grid), jnp.bfloat16),
            pltpu.VMEM((pairs, grid), jnp.bfloat16),
        ],
        compiler_params=pltpu.CompilerParams(vmem_limit_bytes=48 << 20),
        name="densities",
    )(row_orbitals, orbitals, plane_vale, plane_cond)


def images(owner, rank, incoming, vale, cond, vec_tile, row_tile, waves):
    point_local, row_count, pairs, depth = vale.shape
    width = cond.shape[3]
    vec_count = vec_tile.shape[0]
    rest = waves - MAIN

    def kernel(
        owner_ref, rank_ref, block_ref, vale_ref, cond_ref, vec_ref, rowvec_ref, row_out, col_out,
        matrix, row_sum, col_sum,
    ):
        b = pl.program_id(0)
        a = pl.program_id(1)
        pair = b * row_count + a

        @pl.when(pair == 0)
        def _():
            row_sum[...] = jnp.zeros(row_sum.shape, jnp.float32)
            col_sum[...] = jnp.zeros(col_sum.shape, jnp.float32)

        rank = rank_ref[pair]
        density = vale_ref[0, 0]
        main = block_ref[0, :, pl.ds(pl.multiple_of(rank * MAIN, MAIN), MAIN)]
        shared = block_ref[0, :, CAP * MAIN :]
        screened = jnp.dot(density, main, preferred_element_type=jnp.float32).astype(jnp.bfloat16)
        others = jnp.dot(density, shared, preferred_element_type=jnp.float32)
        others = jnp.where(rank == 0, others, pltpu.roll(others, HALF, 1))
        lane = lax.broadcasted_iota(jnp.int32, others.shape, 1)
        others = jnp.where(lane < rest, others, 0.0).astype(jnp.bfloat16)
        nt = (((1,), (1,)), ((), ()))
        matrix[...] = lax.dot_general(
            screened, cond_ref[0, 0, :, :MAIN], nt, preferred_element_type=jnp.float32
        ) + lax.dot_general(
            others, cond_ref[0, 0, :, MAIN:], nt, preferred_element_type=jnp.float32
        )
        for n in range(vec_count):
            vec = vec_ref[n, b]
            total = jnp.zeros((16, pairs), jnp.float32)
            for v in range(16):
                part = matrix[v * 16 : (v + 1) * 16, :]
                term = part * vec
                row_sum[n, a, v] += term[:8] + term[8:]
                total += part * rowvec_ref[n, a, v : v + 1, :]
            col_sum[n, b] += total

        @pl.when(pair == point_local * row_count - 1)
        def _():
            lane_in = lax.broadcasted_iota(jnp.int32, (16, pairs), 1)
            group = lax.broadcasted_iota(jnp.int32, (16, pairs), 0)
            pick_c = jnp.where(lane_in // 16 == group, 1.0, 0.0)
            pick_d = jnp.where(lane_in % 16 == group, 1.0, 0.0)
            rows = jnp.sum(row_sum[...].reshape(-1, 8, pairs), axis=1)
            cols = col_sum[...].reshape(-1, pairs)
            row_out[...] = lax.dot_general(
                pick_c, rows, nt, precision=lax.Precision.HIGHEST, preferred_element_type=jnp.float32
            )
            col_out[...] = lax.dot_general(
                pick_d, cols, nt, precision=lax.Precision.HIGHEST, preferred_element_type=jnp.float32
            )

    whole4 = lambda b, a, o, r: (0, 0, 0, 0)
    whole2 = lambda b, a, o, r: (0, 0)
    row_shape = (NC, vec_count * row_count * NV)
    col_shape = (NC, vec_count * point_local * NV)
    return pl.pallas_call(
        kernel,
        out_shape=(
            jax.ShapeDtypeStruct(row_shape, jnp.float32),
            jax.ShapeDtypeStruct(col_shape, jnp.float32),
        ),
        grid_spec=pltpu.PrefetchScalarGridSpec(
            num_scalar_prefetch=2,
            grid=(point_local, row_count),
            in_specs=[
                pl.BlockSpec((1, depth, WIDE), lambda b, a, o, r: (o[b * row_count + a], 0, 0)),
                pl.BlockSpec((1, 1, pairs, depth), lambda b, a, o, r: (b, a, 0, 0)),
                pl.BlockSpec((1, 1, pairs, width), lambda b, a, o, r: (b, a, 0, 0)),
                pl.BlockSpec(vec_tile.shape, whole4),
                pl.BlockSpec(row_tile.shape, whole4),
            ],
            out_specs=(pl.BlockSpec(row_shape, whole2), pl.BlockSpec(col_shape, whole2)),
            scratch_shapes=[
                pltpu.VMEM((pairs, pairs), jnp.float32),
                pltpu.VMEM((vec_count, row_count, 16, 8, pairs), jnp.float32),
                pltpu.VMEM((vec_count, point_local, 16, pairs), jnp.float32),
            ],
        ),
        compiler_params=pltpu.CompilerParams(vmem_limit_bytes=48 << 20),
        name="images",
    )(owner, rank, incoming, vale, cond, vec_tile, row_tile)


def sum_over(values, axis):
    size = lax.axis_size(axis)
    step = 1
    while step < size:
        perm = [(i, i ^ step) for i in range(size)]
        values = jax.tree.map(lambda x: x + lax.ppermute(x, axis, perm), values)
        step *= 2
    return values


def on_device(row_orbitals, orbitals, screening, pair_blocks, row_vectors, vectors):
    ka_count = lax.axis_size("ka")
    my_point = lax.axis_index("ka")
    my_slice = lax.axis_index("ga")
    row_count = row_orbitals.shape[0]
    point_local, _, grid = orbitals.shape
    block_local, wave_count, slice_width = screening.shape
    pair_count = point_local * row_count
    vec_count = vectors.shape[0]

    flat = pair_blocks.reshape(-1)
    outgoing = gather_blocks(
        flat, my_point.reshape(1), jnp.swapaxes(screening, 1, 2), pair_count
    )
    incoming = lax.all_to_all(outgoing, "ka", split_axis=0, concat_axis=0, tiled=True)

    mine = lax.dynamic_slice_in_dim(flat, my_point * pair_count, pair_count)
    owner = mine // block_local
    order = lax.iota(jnp.int32, pair_count)
    earlier = (owner[:, None] == owner[None, :]) & (order[None, :] < order[:, None])
    rank = jnp.sum(earlier.astype(jnp.int32), axis=1)

    plane_vale = plane_columns(my_slice * slice_width, slice_width, grid, slice_width)
    plane_cond = plane_columns(0, wave_count, grid, MAIN + 2 * HALF)
    vale, cond = densities(
        row_orbitals.astype(jnp.float32), orbitals.astype(jnp.float32), plane_vale, plane_cond
    )
    vec_tile = jnp.tile(
        vectors.astype(jnp.float32).reshape(vec_count, point_local, NV, NC), (1, 1, 1, NC)
    )
    row_tile = jnp.repeat(
        row_vectors.astype(jnp.float32).reshape(vec_count, row_count, NV, NC), NC, axis=3
    )
    row_part, col_part = images(
        owner, rank, incoming, vale, cond, vec_tile, row_tile, wave_count
    )
    row_part, col_part = sum_over((row_part, col_part), "ga")
    row_part = sum_over(row_part, "ka")
    row_scale = float(wave_count * NV * NC * point_local * ka_count) ** (-0.5)
    column_scale = float(wave_count * NV * NC * row_count) ** (-0.5)

    def place(part, count, scale):
        part = part.reshape(NC, vec_count, count, NV) * scale
        return part.transpose(1, 2, 3, 0).reshape(vec_count, count, NV * NC)

    return (
        place(row_part, row_count, row_scale),
        place(col_part, point_local, column_scale),
    )


def solution(mesh):
    return jax.shard_map(
        on_device,
        mesh=mesh,
        in_specs=(P(), P("ka", None, None), P("ka", None, "ga"), P(), P(), P(None, "ka", None)),
        out_specs=(P(), P(None, "ka", None)),
        check_vma=False,
    )
```

```python
import math

import jax
import jax.numpy as jnp
from jax import lax
from jax.experimental import pallas as pl
from jax.experimental.pallas import tpu as pltpu
from jax.sharding import PartitionSpec as P

NV = 16
NC = 16
CAP = 2
SIDES = 2
MAIN = 256
HALF = 64
WIDE = CAP * MAIN + 2 * HALF
WIDE_ONE = MAIN + 2 * HALF
LIMIT = 60 << 20
TAIL = 128
CHUNK = 512
NT = (((1,), (1,)), ((), ()))
VMEM = pl.BlockSpec(memory_space=pltpu.VMEM)
SMEM = pl.BlockSpec(memory_space=pltpu.SMEM)
HBM = pl.BlockSpec(memory_space=pltpu.HBM)


def mirror_of(device, count):
    half = count // SIDES
    return jnp.where(device < half, device + half, device - half)


def gather_blocks(table, blocks, ka_count):
    row_count = table.shape[0]
    point_local = table.shape[1] // ka_count
    block_local, depth, waves = blocks.shape
    rest = waves - MAIN
    half = ka_count // SIDES
    slots = half * SIDES

    def kernel(
        table_hbm, blocks_ref, out_ref, table_ref, held, shared, count, table_sem, in_sem, main_sem,
        shared_sem,
    ):
        me = lax.axis_index("ka")
        base = me * block_local
        first = jnp.where(me < half, 0, half)
        copy = pltpu.make_async_copy(table_hbm, table_ref, table_sem)
        copy.start()
        copy.wait()

        def start(d, carry):
            device = first + lax.rem(d, half)
            device = jnp.where(d < half, device, mirror_of(device, ka_count))
            taken = jnp.int32(0)
            for b in range(point_local):
                for a in range(row_count):
                    local = table_ref[a, device * point_local + b] - base
                    hit = (local >= 0) & (local < block_local) & (taken < CAP)

                    @pl.when(hit)
                    def _():
                        at = d * CAP + taken
                        pltpu.make_async_copy(
                            blocks_ref.at[local], held.at[at], in_sem.at[at]
                        ).start()

                    taken = taken + hit.astype(jnp.int32)
            count[d] = taken
            return carry

        lax.fori_loop(0, slots, start, 0)

        def main_copy(d, s):
            return pltpu.make_async_copy(
                held.at[d * CAP + s, :, pl.ds(0, MAIN)],
                out_ref.at[lax.rem(d, half), d // half, :, pl.ds(s * MAIN, MAIN)],
                main_sem.at[d * CAP + s],
            )

        def shared_copy(d):
            return pltpu.make_async_copy(
                shared.at[d],
                out_ref.at[lax.rem(d, half), d // half, :, pl.ds(CAP * MAIN, 2 * HALF)],
                shared_sem.at[d],
            )

        def pack(d, carry):
            for s in range(CAP):

                @pl.when(count[d] > s)
                def _():
                    at = d * CAP + s
                    pltpu.make_async_copy(blocks_ref.at[0], held.at[at], in_sem.at[at]).wait()
                    main_copy(d, s).start()
                    shared[d, :, s * HALF : s * HALF + rest] = held[at, :, MAIN:]

            @pl.when(count[d] > 0)
            def _():
                shared_copy(d).start()

            return carry

        lax.fori_loop(0, slots, pack, 0)

        def finish(d, carry):
            for s in range(CAP):

                @pl.when(count[d] > s)
                def _():
                    main_copy(d, s).wait()

            @pl.when(count[d] > 0)
            def _():
                shared_copy(d).wait()

            return carry

        lax.fori_loop(0, slots, finish, 0)

    return pl.pallas_call(
        kernel,
        out_shape=jax.ShapeDtypeStruct((half, SIDES, depth, WIDE), jnp.bfloat16),
        in_specs=[HBM, HBM],
        out_specs=HBM,
        scratch_shapes=[
            pltpu.SMEM(table.shape, jnp.int32),
            pltpu.VMEM((slots * CAP, depth, waves), jnp.bfloat16),
            pltpu.VMEM((slots, depth, 2 * HALF), jnp.bfloat16),
            pltpu.SMEM((slots,), jnp.int32),
            pltpu.SemaphoreType.DMA,
            pltpu.SemaphoreType.DMA((slots * CAP,)),
            pltpu.SemaphoreType.DMA((slots * CAP,)),
            pltpu.SemaphoreType.DMA((slots,)),
        ],
        compiler_params=pltpu.CompilerParams(vmem_limit_bytes=LIMIT),
        name="gather_blocks",
    )(table, blocks)


def spread_vectors(vec_ref, keep_second):
    count, pairs = vec_ref.shape
    row = lax.broadcasted_iota(jnp.int32, (count * 16, pairs), 0)
    lane = lax.broadcasted_iota(jnp.int32, (count * 16, pairs), 1)
    values = vec_ref[...].astype(jnp.float32)
    values = jnp.concatenate(
        [jnp.broadcast_to(values[i : i + 1], (16, pairs)) for i in range(count)], axis=0
    )
    values = jnp.where(lane // 16 == row % 16, values, 0.0).astype(jnp.bfloat16)
    at = lax.broadcasted_iota(jnp.int32, (pairs, pairs), 0)
    to = lax.broadcasted_iota(jnp.int32, (pairs, pairs), 1)
    index = to % 16 if keep_second else to // 16
    pick = jnp.where(at % 16 == index, 1.0, 0.0).astype(jnp.bfloat16)
    return jnp.dot(values, pick, preferred_element_type=jnp.float32).reshape(count, 16, pairs)


def densities(side, table, rows, pieces, plane, vecs, sizes):
    ka_count, block_local, depth, waves = sizes
    row_count = table.shape[0]
    point_local = table.shape[1] // ka_count
    pair_count = row_count * point_local
    grid = rows.shape[1]
    mid = grid // 2
    points = mid + TAIL
    width = WIDE_ONE
    half = ka_count // SIDES
    pairs = NV * NV
    block = 256
    n_piece = len(pieces)
    n_vec = len(vecs)
    make_plane = not plane

    def wave(first, step, lanes, count):
        point = lax.broadcasted_iota(jnp.int32, (TAIL, lanes), 0) + step * TAIL
        column = lax.broadcasted_iota(jnp.int32, (TAIL, lanes), 1)
        if lanes == WIDE_ONE:
            column = jnp.where(column < MAIN + HALF, column, column - HALF)
        phase = (first + column) * point
        phase = phase & (grid - 1) if grid & (grid - 1) == 0 else lax.rem(phase, grid)
        away = jnp.abs(phase - grid // 2)
        z = 1.0 - away.astype(jnp.float32) * (4.0 / grid)
        square = z * z
        value = jnp.zeros_like(z)
        for k in (11, 9, 7, 5, 3, 1):
            term = (math.pi / 2) ** k / math.factorial(k) * (-1.0) ** (k // 2)
            value = value * square + term
        value = value * z * (-math.sqrt(2.0 / grid))
        return jnp.where(column < count, value, 0.0).astype(jnp.bfloat16)

    def kernel(*refs):
        refs = list(refs)
        take = lambda count: [refs.pop(0) for _ in range(count)]
        table_hbm, row_hbm = take(2)
        piece_hbm = take(n_piece)
        plane_in = take(0 if make_plane else 2)
        vec_refs = take(n_vec)
        vale_ref, cond_ref, list_ref = take(3)
        vec_out = take(n_vec)
        plane_out = take(2 if make_plane else 0)
        table_ref, row_raw, ket_raw, vplane, cplane = take(5)
        row1, row2, ket1, ket2, fv, fc, vbuf, cbuf, seen = take(9)
        load_sem, out_sem, plane_sem = take(3)

        me = lax.axis_index("ka")
        source = me if side == 0 else mirror_of(me, ka_count)
        first = jnp.where(me < half, 0, half)

        loads = [
            pltpu.make_async_copy(table_hbm, table_ref, load_sem.at[0]),
            pltpu.make_async_copy(row_hbm, row_raw, load_sem.at[1]),
        ]
        low = 0
        for i, ref in enumerate(piece_hbm):
            size = ref.shape[0]
            loads.append(
                pltpu.make_async_copy(ref, ket_raw.at[pl.ds(low, size)], load_sem.at[2 + i])
            )
            low += size
        for i, (ref, to) in enumerate(zip(plane_in, (vplane, cplane))):
            loads.append(pltpu.make_async_copy(ref, to, load_sem.at[4 + i]))
        for load in loads:
            load.start()

        if make_plane:
            low = lax.axis_index("ga") * depth

            def fill(step, carry):
                at = pl.ds(pl.multiple_of(step * TAIL, TAIL), TAIL)
                vplane[at, :] = wave(low, step, depth, depth)
                cplane[at, :] = wave(0, step, width, waves)
                return carry

            lax.fori_loop(0, points // TAIL, fill, 0)
            stores = [
                pltpu.make_async_copy(ref, to, plane_sem.at[i])
                for i, (ref, to) in enumerate(zip((vplane, cplane), plane_out))
            ]
            for store in stores:
                store.start()
        else:
            stores = []

        for i in range(n_vec):
            vec_out[i][...] = spread_vectors(vec_refs[i], i == 0)

        at = lax.broadcasted_iota(jnp.int32, (2 * block, block), 0)
        to = lax.broadcasted_iota(jnp.int32, (2 * block, block), 1)
        flip = ((at < block) & (at + to == block)) | ((at == block) & (to == 0))
        flip = jnp.where(flip, 1.0, 0.0).astype(jnp.bfloat16)

        def fold(src, low, size, put):
            rows_at = slice(low, low + size)
            for j in range(mid // block):
                lanes = slice(j * block, (j + 1) * block)
                put(0, lanes, src[rows_at, lanes].astype(jnp.float32))
                begin = grid - (j + 1) * block
                end = begin + (block if j == 0 else 2 * block)
                turned = jnp.dot(
                    src[rows_at, begin:end], flip[: end - begin], preferred_element_type=jnp.float32
                )
                put(1, lanes, turned)
            lane = lax.broadcasted_iota(jnp.int32, (size, TAIL), 1)
            last = src[rows_at, mid : mid + TAIL].astype(jnp.float32)
            put(0, slice(mid, points), jnp.where(lane == 0, last, 0.0))

        def put_whole(one, two):
            def put(which, lanes, values):
                ref = two if which else one
                ref[:, :, :, lanes] = values.reshape(-1, 2, 16, values.shape[1])

            return put

        def put_part(one, two, kind):
            def put(which, lanes, values):
                ref = two if which else one
                for b in range(point_local):
                    ref[b, kind, :, lanes] = values[b * 16 : (b + 1) * 16]

            return put

        loads[0].wait()
        loads[1].wait()
        fold(row_raw, 0, row_raw.shape[0], put_whole(row1, row2))
        for i in range(n_piece):
            loads[2 + i].wait()
        if n_piece == 1:
            fold(ket_raw, 0, ket_raw.shape[0], put_whole(ket1, ket2))
        else:
            kind = lax.axis_index("ga") % 2
            size = point_local * 16
            fold(ket_raw, 0, size, put_part(ket1, ket2, kind))
            fold(ket_raw, size, size, put_part(ket1, ket2, 1 - kind))
        for load in loads[2 + n_piece :]:
            load.wait()

        for t in range(half):
            seen[t] = 0
        for f in range(4):
            list_ref[f] = 0

        def outputs(p, slot):
            return (
                pltpu.make_async_copy(vbuf.at[slot], vale_ref.at[p], out_sem.at[0, slot]),
                pltpu.make_async_copy(cbuf.at[slot], cond_ref.at[p], out_sem.at[1, slot]),
            )

        def pair(p, carry):
            b = p // row_count
            a = lax.rem(p, row_count)
            owner = table_ref[a, source * point_local + b] // block_local - first

            @pl.when((owner >= 0) & (owner < half))
            def _():
                at = list_ref[0]
                list_ref[1 + 3 * at] = p
                list_ref[2 + 3 * at] = owner
                list_ref[3 + 3 * at] = seen[owner]
                list_ref[0] = at + 1
                seen[owner] = seen[owner] + 1
                slot = lax.rem(at, 2)

                @pl.when(at >= 2)
                def _():
                    for copy in outputs(p, slot):
                        copy.wait()

                for kind, products, plane_ref, out in (
                    (0, fv, vplane, vbuf),
                    (1, fc, cplane, cbuf),
                ):
                    total = None
                    for low in range(0, points, CHUNK):
                        high = min(low + CHUNK, points)
                        for t in range(low, high, 128):
                            lanes = slice(t, t + 128)
                            k1 = ket1[b, kind, :, lanes]
                            k2 = ket2[b, kind, :, lanes] if t < mid else None
                            for c in range(16):
                                value = row1[a, kind, c : c + 1, lanes] * k1
                                if t < mid:
                                    value += row2[a, kind, c : c + 1, lanes] * k2
                                products[c * 16 : (c + 1) * 16, lanes] = value.astype(jnp.bfloat16)
                        part = jnp.dot(
                            products[:, low:high],
                            plane_ref[low:high, :],
                            preferred_element_type=jnp.float32,
                        )
                        total = part if total is None else total + part
                    out[slot] = (total.T if kind else total).astype(jnp.bfloat16)
                for copy in outputs(p, slot):
                    copy.start()

            return carry

        lax.fori_loop(0, pair_count, pair, 0)
        count = list_ref[0]
        for back in (1, 2):

            @pl.when(count >= back)
            def _():
                for copy in outputs(0, lax.rem(count - back, 2)):
                    copy.wait()

        for store in stores:
            store.wait()

    folded = lambda count: pltpu.VMEM((count, 2, 16, points), jnp.float32)
    plane_shapes = [
        jax.ShapeDtypeStruct((points, depth), jnp.bfloat16),
        jax.ShapeDtypeStruct((points, width), jnp.bfloat16),
    ]
    result = pl.pallas_call(
        kernel,
        out_shape=[
            jax.ShapeDtypeStruct((pair_count, pairs, depth), jnp.bfloat16),
            jax.ShapeDtypeStruct((pair_count, width, pairs), jnp.bfloat16),
            jax.ShapeDtypeStruct((1 + 3 * pair_count,), jnp.int32),
        ]
        + [jax.ShapeDtypeStruct((vec.shape[0], 16, pairs), jnp.float32) for vec in vecs]
        + (plane_shapes if make_plane else []),
        in_specs=[HBM] * (2 + n_piece + len(plane)) + [VMEM] * n_vec,
        out_specs=[HBM, HBM, SMEM] + [VMEM] * n_vec + ([HBM, HBM] if make_plane else []),
        scratch_shapes=[
            pltpu.SMEM(table.shape, jnp.int32),
            pltpu.VMEM(rows.shape, jnp.bfloat16),
            pltpu.VMEM((point_local * 32, grid), jnp.bfloat16),
            pltpu.VMEM((points, depth), jnp.bfloat16),
            pltpu.VMEM((points, width), jnp.bfloat16),
            folded(row_count),
            folded(row_count),
            folded(point_local),
            folded(point_local),
            pltpu.VMEM((pairs, points), jnp.bfloat16),
            pltpu.VMEM((pairs, points), jnp.bfloat16),
            pltpu.VMEM((2, pairs, depth), jnp.bfloat16),
            pltpu.VMEM((2, width, pairs), jnp.bfloat16),
            pltpu.SMEM((half,), jnp.int32),
            pltpu.SemaphoreType.DMA((6,)),
            pltpu.SemaphoreType.DMA((2, 2)),
            pltpu.SemaphoreType.DMA((2,)),
        ],
        compiler_params=pltpu.CompilerParams(vmem_limit_bytes=LIMIT),
        cost_estimate=pl.CostEstimate(
            flops=5 * 10**10 if side else 1, bytes_accessed=10**6, transcendentals=0
        ),
        name="densities_mirror" if side else "densities_own",
    )(table, rows, *pieces, *plane, *vecs)
    return result[:3], result[3 : 3 + n_vec], result[3 + n_vec :]


def images(incoming, sides, vecs, row_vec, counts, row_scale, col_scale, wave_count):
    pair_count, pairs, depth = sides[0][0].shape
    width = sides[0][1].shape[1]
    vec_count, row_count, point_local = counts
    rest = wave_count - MAIN
    most = SIDES * pair_count

    def kernel(*refs):
        refs = list(refs)
        take = lambda count: [refs.pop(0) for _ in range(count)]
        (block_ref,) = take(1)
        side_refs = [take(3) for _ in range(SIDES)]
        vec_hbm = take(SIDES)
        rowvec_ref, out_ref = take(2)
        block_buf, vale_buf, cond_buf, vec_buf, even, odd, row_sum, col_sum = take(8)
        main_sem, shared_sem, vale_sem, cond_sem, vec_sem = take(5)

        own_count = side_refs[0][2][0]
        count = own_count + side_refs[1][2][0]

        def copies(k, at, i):
            vale_ref, cond_ref, list_ref = side_refs[k]
            p, owner, rank = (list_ref[1 + 3 * at + f] for f in range(3))
            lanes = pl.ds(pl.multiple_of(rank * MAIN, MAIN), MAIN)
            return (
                pltpu.make_async_copy(vale_ref.at[p], vale_buf.at[i], vale_sem.at[i]),
                pltpu.make_async_copy(
                    block_ref.at[owner, k, :, lanes],
                    block_buf.at[i, :, pl.ds(0, MAIN)],
                    main_sem.at[i],
                ),
                pltpu.make_async_copy(
                    block_ref.at[owner, k, :, pl.ds(CAP * MAIN, 2 * HALF)],
                    block_buf.at[i, :, pl.ds(MAIN, 2 * HALF)],
                    shared_sem.at[i],
                ),
                pltpu.make_async_copy(cond_ref.at[p], cond_buf.at[i], cond_sem.at[i]),
            )

        for k in range(SIDES):

            def start(at, carry):
                for copy in copies(k, at, at + (own_count if k else 0)):
                    copy.start()
                return carry

            lax.fori_loop(0, side_refs[k][2][0], start, 0)

        vec_copies = [
            pltpu.make_async_copy(vec_hbm[k], vec_buf.at[k], vec_sem.at[k]) for k in range(SIDES)
        ]
        for copy in vec_copies:
            copy.start()
        row_sum[...] = jnp.zeros(row_sum.shape, jnp.float32)
        col_sum[...] = jnp.zeros(col_sum.shape, jnp.float32)
        odd[...] = jnp.zeros(odd.shape, jnp.float32)
        for copy in vec_copies:
            copy.wait()

        def field(i, f):
            i = jnp.clip(i, 0, count - 1)
            own = side_refs[0][2][1 + 3 * jnp.minimum(i, pair_count - 1) + f]
            other = side_refs[1][2][1 + 3 * jnp.maximum(i - own_count, 0) + f]
            return jnp.where(i < own_count, own, other)

        def arrived(i):
            for copy in copies(0, 0, i):
                copy.wait()

        def multiply(i, into):
            rank = field(i, 2)
            at = jnp.minimum(i, count - 1)
            screened = jnp.dot(
                vale_buf[at], block_buf[at], preferred_element_type=jnp.float32
            )
            lane = lax.broadcasted_iota(jnp.int32, (1, WIDE_ONE), 1)
            begin = MAIN + rank * HALF
            mine = (lane < MAIN) | ((lane >= begin) & (lane < begin + rest))
            screened = jnp.where(mine, screened, 0.0).astype(jnp.bfloat16)
            matrix = jnp.dot(screened, cond_buf[at], preferred_element_type=jnp.float32)
            into[...] = jnp.where(i < count, matrix, 0.0)

        def contract(i, matrix):
            p = field(i, 0)
            k = (jnp.clip(i, 0, count - 1) >= own_count).astype(jnp.int32)
            b = p // row_count
            a = lax.rem(p, row_count)
            totals = [jnp.zeros((16, pairs), jnp.float32)] * vec_count
            ket = [vec_buf[k, n * point_local + b] for n in range(vec_count)]
            for v in range(16):
                part = matrix[v * 16 : (v + 1) * 16, :]
                for n in range(vec_count):
                    term = part * ket[n]
                    row_sum[a, n, v] += term[:8] + term[8:]
                    totals[n] += part * rowvec_ref[n * row_count + a, v : v + 1, :]
            for n in range(vec_count):
                col_sum[k, n, b] += totals[n]

        def two(j, carry):
            arrived(2 * j)

            @pl.when(2 * j + 1 < count)
            def _():
                arrived(2 * j + 1)

            multiply(2 * j, even)
            contract(2 * j - 1, odd)
            multiply(2 * j + 1, odd)
            contract(2 * j, even)
            return carry

        trips = (count + 1) // 2
        lax.fori_loop(0, trips, two, 0)

        @pl.when(count > 0)
        def _():
            contract(2 * trips - 1, odd)

        def spread(values, keep_first, scale):
            at = lax.broadcasted_iota(jnp.int32, (pairs, pairs), 0)
            to = lax.broadcasted_iota(jnp.int32, (pairs, pairs), 1)
            index = at // 16 if keep_first else at % 16
            pick = jnp.where(index == to % 16, 1.0, 0.0).astype(jnp.bfloat16)
            high = values.astype(jnp.bfloat16)
            low = (values - high.astype(jnp.float32)).astype(jnp.bfloat16)
            wide = jnp.dot(high, pick, preferred_element_type=jnp.float32) + jnp.dot(
                low, pick, preferred_element_type=jnp.float32
            )
            row = lax.broadcasted_iota(jnp.int32, wide.shape, 0)
            lane = lax.broadcasted_iota(jnp.int32, wide.shape, 1)
            wide = jnp.where(row % 16 == lane // 16, wide, 0.0)
            return jnp.sum(wide.reshape(-1, 16, pairs), axis=1) * scale

        cols = vec_count * point_local
        rows = vec_count * row_count
        columns = spread(col_sum[...].reshape(-1, pairs), False, col_scale)
        out_ref[:cols] = columns[:cols]
        out_ref[cols + rows :] = columns[cols:]
        summed = jnp.sum(row_sum[...].reshape(-1, 8, pairs), axis=1)
        out_ref[cols : cols + rows] = spread(summed, True, row_scale)

    total = vec_count * (SIDES * point_local + row_count)
    return pl.pallas_call(
        kernel,
        out_shape=jax.ShapeDtypeStruct((total, pairs), jnp.float32),
        in_specs=[HBM] + [HBM, HBM, SMEM] * SIDES + [HBM] * SIDES + [VMEM],
        out_specs=VMEM,
        scratch_shapes=[
            pltpu.VMEM((most, depth, WIDE_ONE), jnp.bfloat16),
            pltpu.VMEM((most, pairs, depth), jnp.bfloat16),
            pltpu.VMEM((most, width, pairs), jnp.bfloat16),
            pltpu.VMEM((SIDES,) + vecs[0].shape, jnp.float32),
            pltpu.VMEM((pairs, pairs), jnp.float32),
            pltpu.VMEM((pairs, pairs), jnp.float32),
            pltpu.VMEM((row_count, vec_count, 16, 8, pairs), jnp.float32),
            pltpu.VMEM((SIDES, vec_count, point_local, 16, pairs), jnp.float32),
        ]
        + [pltpu.SemaphoreType.DMA((most,))] * 4
        + [pltpu.SemaphoreType.DMA((SIDES,))],
        compiler_params=pltpu.CompilerParams(vmem_limit_bytes=LIMIT),
        name="images",
    )(incoming, *sides[0], *sides[1], *vecs, row_vec)


def swap(values, axis, step):
    perm = [(i, i ^ step) for i in range(lax.axis_size(axis))]
    return lax.ppermute(values, axis, perm)


def on_device(row_orbitals, orbitals, screening, pair_blocks, row_vectors, vectors):
    ka_count = lax.axis_size("ka")
    ga_count = lax.axis_size("ga")
    half = ka_count // SIDES
    row_count = row_orbitals.shape[0]
    point_local, bands, grid = orbitals.shape
    block_local, wave_count, slice_width = screening.shape
    vec_count = vectors.shape[0]

    kind = lax.axis_index("ga") % 2
    part = lax.dynamic_slice_in_dim(orbitals, kind * NV, NV, 1)
    part = part.reshape(point_local * NV, grid)
    fetched = swap(part, "ka", half)
    mirror_vectors = swap(vectors, "ka", half)

    table = pair_blocks.T
    outgoing = gather_blocks(table, jnp.swapaxes(screening, 1, 2), ka_count)
    outgoing, table = lax.optimization_barrier((outgoing, table))
    groups = [list(range(half)), list(range(half, ka_count))]
    incoming = lax.all_to_all(
        outgoing, "ka", split_axis=0, concat_axis=0, tiled=True, axis_index_groups=groups
    )

    rows = row_orbitals.reshape(row_count * bands, grid)
    sizes = (ka_count, block_local, slice_width, wave_count)
    flat = lambda values: values.reshape(-1, NV * NC)
    own, (own_vec, row_vec), plane = densities(
        0,
        table,
        rows,
        (orbitals.reshape(point_local * bands, grid),),
        (),
        (flat(vectors), flat(row_vectors)),
        sizes,
    )
    fetched, own_vec = lax.optimization_barrier((fetched, own_vec))
    passed = swap(fetched, "ga", 1)
    mirrored, (mirror_vec,), _ = densities(
        1, table, rows, (fetched, passed), plane, (flat(mirror_vectors),), sizes
    )
    row_scale = float(wave_count * NV * NC * point_local * ka_count) ** (-0.5)
    col_scale = float(wave_count * NV * NC * row_count) ** (-0.5)
    part = images(
        incoming,
        (own, mirrored),
        (own_vec, mirror_vec),
        row_vec,
        (vec_count, row_count, point_local),
        row_scale,
        col_scale,
        wave_count,
    )
    step = 1
    while step < ga_count:
        part = part + swap(part, "ga", step)
        step *= 2
    cols = vec_count * point_local
    column = part[:cols]
    row = part[cols:]
    other = swap(row, "ka", half)
    column = column + other[-cols:]
    row = row[:-cols] + other[:-cols]
    step = 1
    while step < half:
        row = row + swap(row, "ka", step)
        step *= 2
    row = row.reshape(row_count, vec_count, NV * NC).transpose(1, 0, 2)
    return row, column.reshape(vec_count, point_local, NV * NC)


def solution(mesh):
    return jax.shard_map(
        on_device,
        mesh=mesh,
        in_specs=(P(), P("ka", None, None), P("ka", None, "ga"), P(), P(), P(None, "ka", None)),
        out_specs=(P(), P(None, "ka", None)),
        check_vma=False,
    )
```

```python
import math

import jax
import jax.numpy as jnp
from jax import lax
from jax.experimental import pallas as pl
from jax.experimental.pallas import tpu as pltpu
from jax.sharding import PartitionSpec as P

NV = 16
NC = 16
CAP = 2
SIDES = 2
MAIN = 256
HALF = 64
WIDE = CAP * MAIN + 2 * HALF
WIDE_ONE = MAIN + 2 * HALF
AHEAD = 4
GROUP = 2
LIMIT = 62 << 20
TAIL = 128
CHUNK = 512
NT = (((1,), (1,)), ((), ()))
VMEM = pl.BlockSpec(memory_space=pltpu.VMEM)
SMEM = pl.BlockSpec(memory_space=pltpu.SMEM)
HBM = pl.BlockSpec(memory_space=pltpu.HBM)


def mirror_of(device, count):
    half = count // SIDES
    return jnp.where(device < half, device + half, device - half)


def gather_blocks(table, blocks, ka_count):
    row_count = table.shape[0]
    point_local = table.shape[1] // ka_count
    block_local, depth, waves = blocks.shape
    rest = waves - MAIN
    half = ka_count // SIDES
    slots = half * SIDES

    def kernel(
        table_hbm, blocks_ref, out_ref, table_ref, held, shared, count, table_sem, in_sem, main_sem,
        shared_sem,
    ):
        me = lax.axis_index("ka")
        base = me * block_local
        first = jnp.where(me < half, 0, half)
        copy = pltpu.make_async_copy(table_hbm, table_ref, table_sem)
        copy.start()
        copy.wait()

        def start(d, carry):
            device = first + lax.rem(d, half)
            device = jnp.where(d < half, device, mirror_of(device, ka_count))
            taken = jnp.int32(0)
            for b in range(point_local):
                for a in range(row_count):
                    local = table_ref[a, device * point_local + b] - base
                    hit = (local >= 0) & (local < block_local) & (taken < CAP)

                    @pl.when(hit)
                    def _():
                        at = d * CAP + taken
                        pltpu.make_async_copy(
                            blocks_ref.at[local], held.at[at], in_sem.at[at]
                        ).start()

                    taken = taken + hit.astype(jnp.int32)
            count[d] = taken
            return carry

        lax.fori_loop(0, slots, start, 0)

        def main_copy(d, s):
            return pltpu.make_async_copy(
                held.at[d * CAP + s, :, pl.ds(0, MAIN)],
                out_ref.at[lax.rem(d, half), d // half, :, pl.ds(s * MAIN, MAIN)],
                main_sem.at[d * CAP + s],
            )

        def shared_copy(d):
            return pltpu.make_async_copy(
                shared.at[d],
                out_ref.at[lax.rem(d, half), d // half, :, pl.ds(CAP * MAIN, 2 * HALF)],
                shared_sem.at[d],
            )

        def pack(d, carry):
            for s in range(CAP):

                @pl.when(count[d] > s)
                def _():
                    at = d * CAP + s
                    pltpu.make_async_copy(blocks_ref.at[0], held.at[at], in_sem.at[at]).wait()
                    main_copy(d, s).start()
                    shared[d, :, s * HALF : s * HALF + rest] = held[at, :, MAIN:]

            @pl.when(count[d] > 0)
            def _():
                shared_copy(d).start()

            return carry

        lax.fori_loop(0, slots, pack, 0)

        def finish(d, carry):
            for s in range(CAP):

                @pl.when(count[d] > s)
                def _():
                    main_copy(d, s).wait()

            @pl.when(count[d] > 0)
            def _():
                shared_copy(d).wait()

            return carry

        lax.fori_loop(0, slots, finish, 0)

    return pl.pallas_call(
        kernel,
        out_shape=jax.ShapeDtypeStruct((half, SIDES, depth, WIDE), jnp.bfloat16),
        in_specs=[HBM, HBM],
        out_specs=HBM,
        scratch_shapes=[
            pltpu.SMEM(table.shape, jnp.int32),
            pltpu.VMEM((slots * CAP, depth, waves), jnp.bfloat16),
            pltpu.VMEM((slots, depth, 2 * HALF), jnp.bfloat16),
            pltpu.SMEM((slots,), jnp.int32),
            pltpu.SemaphoreType.DMA,
            pltpu.SemaphoreType.DMA((slots * CAP,)),
            pltpu.SemaphoreType.DMA((slots * CAP,)),
            pltpu.SemaphoreType.DMA((slots,)),
        ],
        compiler_params=pltpu.CompilerParams(vmem_limit_bytes=LIMIT),
        name="gather_blocks",
    )(table, blocks)


def spread_vectors(vec_ref, keep_second):
    count, pairs = vec_ref.shape
    row = lax.broadcasted_iota(jnp.int32, (count * 16, pairs), 0)
    lane = lax.broadcasted_iota(jnp.int32, (count * 16, pairs), 1)
    values = vec_ref[...].astype(jnp.float32)
    values = jnp.concatenate(
        [jnp.broadcast_to(values[i : i + 1], (16, pairs)) for i in range(count)], axis=0
    )
    values = jnp.where(lane // 16 == row % 16, values, 0.0).astype(jnp.bfloat16)
    at = lax.broadcasted_iota(jnp.int32, (pairs, pairs), 0)
    to = lax.broadcasted_iota(jnp.int32, (pairs, pairs), 1)
    index = to % 16 if keep_second else to // 16
    pick = jnp.where(at % 16 == index, 1.0, 0.0).astype(jnp.bfloat16)
    return jnp.dot(values, pick, preferred_element_type=jnp.float32).reshape(count, 16, pairs)


def densities(side, table, rows, pieces, plane, vecs, sizes):
    ka_count, block_local, depth, waves, vec_rows = sizes
    row_count = table.shape[0]
    point_local = table.shape[1] // ka_count
    pair_count = row_count * point_local
    grid = pieces[0].shape[1] - (NV * NC if plane else 0)
    quarter = grid // 4
    segment = quarter + TAIL
    points = segment + quarter
    width = WIDE_ONE
    evens, odds = (waves + 1) // 2, waves // 2
    half = ka_count // SIDES
    pairs = NV * NV
    block = 256
    n_piece = len(pieces)
    n_vec = len(vecs) + (1 if plane else 0)
    make_plane = not plane

    def cosine(phase):
        phase = phase & (grid - 1) if grid & (grid - 1) == 0 else jnp.remainder(phase, grid)
        away = jnp.abs(phase - grid // 2)
        z = 1.0 - away.astype(jnp.float32) * (4.0 / grid)
        square = z * z
        value = jnp.zeros_like(z)
        for k in (11, 9, 7, 5, 3, 1):
            term = (math.pi / 2) ** k / math.factorial(k) * (-1.0) ** (k // 2)
            value = value * square + term
        return value * -z

    def waves_of(shape):
        lane = lax.broadcasted_iota(jnp.int32, shape, 1)
        parity = (lane >= 2 * MAIN).astype(jnp.int32)
        column = lane - MAIN - parity * MAIN
        wave = jnp.where(
            lane < MAIN, lane + lax.axis_index("ga") * depth, 2 * column + parity
        )
        return wave, (lane < depth) | ((lane >= MAIN) & (column >= 0) & (wave < waves))

    def kernel(*refs):
        refs = list(refs)
        take = lambda count: [refs.pop(0) for _ in range(count)]
        (table_hbm,) = take(1)
        row_hbm = take(1)[0] if make_plane else None
        piece_hbm = take(n_piece)
        plane_in = take(0 if make_plane else 4)
        vec_refs = take(len(vecs))
        vale_ref, cond_ref, list_ref = take(3)
        vec_out = take(n_vec)
        plane_out = take(4 if make_plane else 0)
        table_ref, ket_raw, vplane, eplane, oplane = take(5)
        row_raw, cos_part, sin_part = take(3 if make_plane else 0) or (None,) * 3
        vec_raw = None if make_plane else take(1)[0]
        bras, kets, fv, fe, fo, natural, vbuf, cbuf, seen = take(9)
        load_sem, out_sem, plane_sem = take(3)

        me = lax.axis_index("ka")
        source = me if side == 0 else mirror_of(me, ka_count)
        first = jnp.where(me < half, 0, half)

        loads = [pltpu.make_async_copy(table_hbm, table_ref, load_sem.at[0])]
        if make_plane:
            loads.append(pltpu.make_async_copy(row_hbm, row_raw, load_sem.at[1]))
        ready = len(loads)
        low = 0
        for i, ref in enumerate(piece_hbm):
            size = ref.shape[0]
            loads.append(
                pltpu.make_async_copy(
                    ref.at[:, pl.ds(0, grid)], ket_raw.at[pl.ds(low, size)], load_sem.at[2 + i]
                )
            )
            low += size
        for i, (ref, to) in enumerate(zip(plane_in, (vplane, eplane, oplane, bras))):
            loads.append(pltpu.make_async_copy(ref, to, load_sem.at[4 + i]))
        if not make_plane:
            loads.append(
                pltpu.make_async_copy(
                    piece_hbm[0].at[pl.ds(0, vec_raw.shape[0]), pl.ds(grid, pairs)],
                    vec_raw,
                    load_sem.at[8],
                )
            )
            vec_refs = [vec_raw]
        for load in loads:
            load.start()

        if make_plane:
            wave, valid = waves_of(cos_part.shape)
            point = lax.broadcasted_iota(jnp.int32, cos_part.shape, 0)
            scale = jnp.where(valid, math.sqrt(2.0 / grid), 0.0)
            cos_part[...] = cosine(wave * point) * scale
            sin_part[...] = cosine(wave * point - grid // 4) * scale
            wave8, _ = waves_of((8, cos_part.shape[1]))

            def fill(step, carry):
                at = pl.ds(pl.multiple_of(step * TAIL, TAIL), TAIL)
                turn = wave8 * (step * TAIL)
                value = cosine(turn)[:1] * cos_part[...]
                value -= cosine(turn - grid // 4)[:1] * sin_part[...]
                value = value.astype(jnp.bfloat16)
                vplane[at, :] = value[:, :depth]
                eplane[at, :] = value[:, MAIN : MAIN + evens]
                oplane[at, :] = value[:, 2 * MAIN : 2 * MAIN + odds]
                return carry

            def fill_back(step, carry):
                at = pl.ds(pl.multiple_of(segment + step * TAIL, TAIL), TAIL)
                turn = wave8[:, :MAIN] * (grid // 2 - step * TAIL)
                value = cosine(turn)[:1] * cos_part[:, :MAIN]
                value += cosine(turn - grid // 4)[:1] * sin_part[:, :MAIN]
                vplane[at, :] = value.astype(jnp.bfloat16)[:, :depth]
                return carry

            lax.fori_loop(0, segment // TAIL, fill, 0)
            lax.fori_loop(0, quarter // TAIL, fill_back, 0)

        at = lax.broadcasted_iota(jnp.int32, (2 * block, block), 0)
        to = lax.broadcasted_iota(jnp.int32, (2 * block, block), 1)
        flip = ((at < block) & (at + to == block)) | ((at == block) & (to == 0))
        flip = jnp.where(flip, 1.0, 0.0).astype(jnp.bfloat16)

        def fold(src, low, size, put):
            rows_at = slice(low, low + size)
            lane = lax.broadcasted_iota(jnp.int32, (size, block), 1)

            def turned(begin, end):
                return jnp.dot(
                    src[rows_at, begin:end], flip[: end - begin], preferred_element_type=jnp.float32
                )

            for at in range(0, quarter, block):
                end = grid - at - block
                there = src[rows_at, grid // 2 + at : grid // 2 + at + block].astype(jnp.float32)
                parts = (
                    src[rows_at, at : at + block].astype(jnp.float32),
                    turned(end, min(end + 2 * block, grid)),
                    turned(end - grid // 2, end - grid // 2 + 2 * block),
                    there if at else jnp.where(lane == 0, 0.0, there),
                )
                for k, values in enumerate(parts):
                    put(slice(k * segment + at, k * segment + at + block), values)
            for k in range(2):
                at = (2 * k + 1) * quarter
                last = src[rows_at, at : at + TAIL].astype(jnp.float32)
                at = k * segment + quarter
                put(slice(at, at + TAIL), jnp.where(lane[:, :TAIL] == 0, last, 0.0))

        def put_whole(ref):
            def put(lanes, values):
                ref[:, :, :, lanes] = values.reshape(-1, 2, 16, values.shape[1])

            return put

        def put_part(ref, kind):
            def put(lanes, values):
                for b in range(point_local):
                    ref[b, kind, :, lanes] = values[b * 16 : (b + 1) * 16]

            return put

        stores = []
        if make_plane:
            loads[1].wait()
            fold(row_raw, 0, row_raw.shape[0], put_whole(bras))
            stores = [
                pltpu.make_async_copy(ref, to, plane_sem.at[i])
                for i, (ref, to) in enumerate(zip((vplane, eplane, oplane, bras), plane_out))
            ]
            for store in stores:
                store.start()
        for i in range(n_piece):
            loads[ready + i].wait()
        if n_piece == 1:
            fold(ket_raw, 0, ket_raw.shape[0], put_whole(kets))
        else:
            kind = lax.axis_index("ga") % 2
            size = point_local * 16
            fold(ket_raw, 0, size, put_part(kets, kind))
            fold(ket_raw, size, size, put_part(kets, 1 - kind))
        for load in loads[:1] + loads[ready + n_piece :]:
            load.wait()
        for i in range(n_vec):
            vec_out[i][...] = spread_vectors(vec_refs[i], i == 0)

        for t in range(half):
            seen[t] = 0
        for f in range(4):
            list_ref[f] = 0

        def listed(p, carry):
            b = p // row_count
            a = lax.rem(p, row_count)
            owner = table_ref[a, source * point_local + b] // block_local - first

            @pl.when((owner >= 0) & (owner < half))
            def _():
                at = list_ref[0]
                list_ref[1 + 3 * at] = p
                list_ref[2 + 3 * at] = owner
                list_ref[3 + 3 * at] = seen[owner]
                list_ref[0] = at + 1
                seen[owner] = seen[owner] + 1

            return carry

        lax.fori_loop(0, pair_count, listed, 0)
        count = list_ref[0]

        def outputs(n, g):
            slot = lax.rem(n, 2)
            p = list_ref[1 + 3 * jnp.minimum(n * GROUP + g, pair_count - 1)]
            return (
                pltpu.make_async_copy(vbuf.at[slot, g], vale_ref.at[p], out_sem.at[slot, g, 0]),
                pltpu.make_async_copy(cbuf.at[slot, g], cond_ref.at[p], out_sem.at[slot, g, 1]),
            )

        def finish(n):
            for g in range(GROUP):

                @pl.when((n >= 0) & (n * GROUP + g < count))
                def _():
                    for copy in outputs(n, g):
                        copy.wait()

        def group(n, carry):
            finish(n - 2)
            slot = lax.rem(n, 2)
            entries = [list_ref[1 + 3 * jnp.minimum(n * GROUP + g, count - 1)] for g in range(GROUP)]
            places = [(lax.rem(p, row_count), p // row_count) for p in entries]

            def products(kind, t):
                spans = range(4 if t < quarter else 2)
                lanes = [slice(k * segment + t, k * segment + t + 128) for k in spans]
                for g, (a, b) in enumerate(places):
                    ket = [kets[b, kind, :, at] for at in lanes]
                    for c in range(16):
                        bra = [bras[a, kind, c : c + 1, at] for at in lanes]
                        row = g * pairs + c * 16
                        yield slice(row, row + 16), [
                            bra[k] * ket[k] + bra[k + 1] * ket[k + 1] for k in spans[::2]
                        ]

            def times(lhs, low, high, plane_ref, total):
                part = jnp.dot(
                    lhs[:, low:high], plane_ref[low:high, :], preferred_element_type=jnp.float32
                )
                return part if total is None else total + part

            sums = {"vale": None, "even": None, "odd": None}

            def cond_products(low, high):
                for t in range(low, high, 128):
                    for at, value in products(1, t):
                        if t < quarter:
                            fe[at, t : t + 128] = (value[0] + value[1]).astype(jnp.bfloat16)
                            fo[at, t : t + 128] = (value[0] - value[1]).astype(jnp.bfloat16)
                        else:
                            fe[at, t : t + 128] = value[0].astype(jnp.bfloat16)

            def cond_sums(low, high):
                sums["even"] = times(fe, low, high, eplane, sums["even"])
                if low < quarter:
                    sums["odd"] = times(fo, low, high, oplane, sums["odd"])

            def vale_products(low, high):
                for t in range(low, high, 128):
                    for at, value in products(0, t):
                        for k, part in enumerate(value):
                            to = k * segment + t
                            fv[at, to : to + 128] = part.astype(jnp.bfloat16)

            def vale_sums(low, high):
                sums["vale"] = times(fv, low, high, vplane, sums["vale"])
                if low < quarter:
                    sums["vale"] = times(fv, segment + low, segment + high, vplane, sums["vale"])

            def cond_out():
                rest = waves - MAIN
                blank = jnp.zeros((HALF - rest, pairs), jnp.bfloat16)
                for g in range(GROUP):
                    for h in range(pairs // 128):
                        rows_at = slice(g * pairs + h * 128, g * pairs + (h + 1) * 128)
                        lanes = slice(h * 128, (h + 1) * 128)
                        natural[h, pl.ds(0, evens, stride=2), :] = sums["even"][rows_at].T
                        natural[h, pl.ds(1, odds, stride=2), :] = sums["odd"][rows_at].T
                        cbuf[slot, g, :waves, lanes] = natural[h, :waves].astype(jnp.bfloat16)
                        cbuf[slot, g, MAIN + HALF : waves + HALF, lanes] = natural[
                            h, MAIN:waves
                        ].astype(jnp.bfloat16)
                    cbuf[slot, g, waves : MAIN + HALF] = blank
                    cbuf[slot, g, waves + HALF :] = blank

            chunks = [(low, min(low + CHUNK, segment)) for low in range(0, segment, CHUNK)]
            steps = [(cond_products, cond_sums, chunk) for chunk in chunks]
            steps += [(vale_products, vale_sums, chunk) for chunk in chunks]
            steps[0][0](*steps[0][2])
            for at, (_, add, chunk) in enumerate(steps):
                if at + 1 < len(steps):
                    steps[at + 1][0](*steps[at + 1][2])
                add(*chunk)
                if at == len(chunks):
                    cond_out()
            vbuf[slot] = sums["vale"].astype(jnp.bfloat16).reshape(GROUP, pairs, depth)
            for g in range(GROUP):

                @pl.when(n * GROUP + g < count)
                def _():
                    for copy in outputs(n, g):
                        copy.start()

            return carry

        trips = (count + GROUP - 1) // GROUP
        lax.fori_loop(0, trips, group, 0)
        finish(trips - 2)
        finish(trips - 1)
        for store in stores:
            store.wait()

    folded = lambda count: pltpu.VMEM((count, 2, 16, 4 * segment), jnp.float32)
    plane_shapes = [
        jax.ShapeDtypeStruct((points, depth), jnp.bfloat16),
        jax.ShapeDtypeStruct((segment, evens), jnp.bfloat16),
        jax.ShapeDtypeStruct((segment, odds), jnp.bfloat16),
        jax.ShapeDtypeStruct((row_count, 2, 16, 4 * segment), jnp.float32),
    ]
    result = pl.pallas_call(
        kernel,
        out_shape=[
            jax.ShapeDtypeStruct((pair_count, pairs, depth), jnp.bfloat16),
            jax.ShapeDtypeStruct((pair_count, width, pairs), jnp.bfloat16),
            jax.ShapeDtypeStruct((1 + 3 * pair_count,), jnp.int32),
        ]
        + [jax.ShapeDtypeStruct((vec_rows, 16, pairs), jnp.float32)] * n_vec
        + (plane_shapes if make_plane else []),
        in_specs=[HBM] * (1 + len(rows) + n_piece + len(plane)) + [VMEM] * len(vecs),
        out_specs=[HBM, HBM, SMEM] + [VMEM] * n_vec + ([HBM] * 4 if make_plane else []),
        scratch_shapes=[
            pltpu.SMEM(table.shape, jnp.int32),
            pltpu.VMEM((point_local * 32, grid), jnp.bfloat16),
            pltpu.VMEM((points, depth), jnp.bfloat16),
            pltpu.VMEM((segment, evens), jnp.bfloat16),
            pltpu.VMEM((segment, odds), jnp.bfloat16),
        ]
        + (
            [
                pltpu.VMEM(rows[0].shape, jnp.bfloat16),
                pltpu.VMEM((TAIL, 3 * MAIN), jnp.float32),
                pltpu.VMEM((TAIL, 3 * MAIN), jnp.float32),
            ]
            if make_plane
            else [pltpu.VMEM((vec_rows, pairs), jnp.bfloat16)]
        )
        + [
            folded(row_count),
            folded(point_local),
            pltpu.VMEM((GROUP * pairs, points), jnp.bfloat16),
            pltpu.VMEM((GROUP * pairs, segment), jnp.bfloat16),
            pltpu.VMEM((GROUP * pairs, quarter), jnp.bfloat16),
            pltpu.VMEM((pairs // 128, 2 * evens, 128), jnp.float32),
            pltpu.VMEM((2, GROUP, pairs, depth), jnp.bfloat16),
            pltpu.VMEM((2, GROUP, width, pairs), jnp.bfloat16),
            pltpu.SMEM((half,), jnp.int32),
            pltpu.SemaphoreType.DMA((9,)),
            pltpu.SemaphoreType.DMA((2, GROUP, 2)),
            pltpu.SemaphoreType.DMA((4,)),
        ],
        compiler_params=pltpu.CompilerParams(vmem_limit_bytes=LIMIT),
        cost_estimate=pl.CostEstimate(
            flops=5 * 10**10 if side else 1, bytes_accessed=10**6, transcendentals=0
        ),
        name="densities_mirror" if side else "densities_own",
    )(table, *rows, *pieces, *plane, *vecs)
    return result[:3], result[3 : 3 + n_vec], result[3 + n_vec :]


def images(incoming, sides, vecs, row_vec, counts, row_scale, col_scale, wave_count):
    pair_count, pairs, depth = sides[0][0].shape
    width = sides[0][1].shape[1]
    vec_count, row_count, point_local = counts
    rest = wave_count - MAIN
    most = SIDES * pair_count

    def kernel(*refs):
        refs = list(refs)
        take = lambda count: [refs.pop(0) for _ in range(count)]
        (block_ref,) = take(1)
        side_refs = [take(3) for _ in range(SIDES)]
        vec_hbm = take(SIDES)
        rowvec_hbm, out_ref = take(2)
        block_buf, vale_buf, cond_buf, vec_buf, rowvec_ref, even, odd, row_sum, col_sum = take(9)
        main_sem, shared_sem, vale_sem, cond_sem, vec_sem = take(5)

        own_count = side_refs[0][2][0]
        count = own_count + side_refs[1][2][0]

        def field(i, f):
            i = jnp.clip(i, 0, count - 1)
            own = side_refs[0][2][1 + 3 * jnp.minimum(i, pair_count - 1) + f]
            other = side_refs[1][2][1 + 3 * jnp.maximum(i - own_count, 0) + f]
            return jnp.where(i < own_count, own, other)

        def copies(k, i):
            vale_ref, cond_ref, _ = side_refs[k]
            p, owner, rank = (field(i, f) for f in range(3))
            lanes = pl.ds(pl.multiple_of(rank * MAIN, MAIN), MAIN)
            return (
                pltpu.make_async_copy(vale_ref.at[p], vale_buf.at[i], vale_sem.at[i]),
                pltpu.make_async_copy(
                    block_ref.at[owner, k, :, lanes],
                    block_buf.at[i, :, pl.ds(0, MAIN)],
                    main_sem.at[i],
                ),
                pltpu.make_async_copy(
                    block_ref.at[owner, k, :, pl.ds(CAP * MAIN, 2 * HALF)],
                    block_buf.at[i, :, pl.ds(MAIN, 2 * HALF)],
                    shared_sem.at[i],
                ),
                pltpu.make_async_copy(cond_ref.at[p], cond_buf.at[i], cond_sem.at[i]),
            )

        def start(i):
            for k in range(SIDES):
                low = own_count if k else 0
                high = count if k else own_count

                @pl.when((i >= low) & (i < high))
                def _():
                    for copy in copies(k, i):
                        copy.start()

        def arrived(i):
            for copy in copies(0, i):
                copy.wait()

        for i in range(AHEAD):
            start(i)
        vec_copies = [
            pltpu.make_async_copy(ref, to, vec_sem.at[k])
            for k, (ref, to) in enumerate(
                [(rowvec_hbm, rowvec_ref)] + [(vec_hbm[k], vec_buf.at[k]) for k in range(SIDES)]
            )
        ]
        for copy in vec_copies:
            copy.start()
        row_sum[...] = jnp.zeros(row_sum.shape, jnp.float32)
        col_sum[...] = jnp.zeros(col_sum.shape, jnp.float32)
        odd[...] = jnp.zeros(odd.shape, jnp.float32)
        for copy in vec_copies:
            copy.wait()

        def screen(i):
            at = jnp.minimum(i, count - 1)
            screened = jnp.dot(
                vale_buf[at], block_buf[at], preferred_element_type=jnp.float32
            )
            lane = lax.broadcasted_iota(jnp.int32, (1, WIDE_ONE), 1)
            begin = MAIN + field(i, 2) * HALF
            mine = (lane < MAIN) | ((lane >= begin) & (lane < begin + rest))
            return jnp.where(mine & (i < count), screened, 0.0).astype(jnp.bfloat16)

        def multiply(i, screened, into):
            at = jnp.minimum(i, count - 1)
            into[...] = jnp.dot(screened, cond_buf[at], preferred_element_type=jnp.float32)

        def contract(i, matrix):
            p = field(i, 0)
            k = (jnp.clip(i, 0, count - 1) >= own_count).astype(jnp.int32)
            b = p // row_count
            a = lax.rem(p, row_count)
            totals = [jnp.zeros((16, pairs), jnp.float32)] * vec_count
            ket = [vec_buf[k, n * point_local + b] for n in range(vec_count)]
            for v in range(16):
                part = matrix[v * 16 : (v + 1) * 16, :]
                for n in range(vec_count):
                    term = part * ket[n]
                    row_sum[n, a, v] += term[:8] + term[8:]
                    totals[n] += part * rowvec_ref[n * row_count + a, v : v + 1, :]
            for n in range(vec_count):
                col_sum[k, n, b] += totals[n]

        def two(j, carry):
            for i in range(2):
                start(2 * j + AHEAD + i)
            arrived(2 * j)

            @pl.when(2 * j + 1 < count)
            def _():
                arrived(2 * j + 1)

            first = screen(2 * j)
            second = screen(2 * j + 1)
            contract(2 * j - 1, odd)
            multiply(2 * j, first, even)
            multiply(2 * j + 1, second, odd)
            contract(2 * j, even)
            return carry

        trips = (count + 1) // 2
        lax.fori_loop(0, trips, two, 0)

        @pl.when(count > 0)
        def _():
            contract(2 * trips - 1, odd)

        def spread(values, keep_first, scale):
            at = lax.broadcasted_iota(jnp.int32, (pairs, pairs), 0)
            to = lax.broadcasted_iota(jnp.int32, (pairs, pairs), 1)
            index = at // 16 if keep_first else at % 16
            pick = jnp.where(index == to % 16, 1.0, 0.0).astype(jnp.bfloat16)
            high = values.astype(jnp.bfloat16)
            low = (values - high.astype(jnp.float32)).astype(jnp.bfloat16)
            wide = jnp.dot(high, pick, preferred_element_type=jnp.float32) + jnp.dot(
                low, pick, preferred_element_type=jnp.float32
            )
            row = lax.broadcasted_iota(jnp.int32, wide.shape, 0)
            lane = lax.broadcasted_iota(jnp.int32, wide.shape, 1)
            wide = jnp.where(row % 16 == lane // 16, wide, 0.0)
            return jnp.sum(wide.reshape(-1, 16, pairs), axis=1) * scale

        columns = spread(col_sum[...].reshape(-1, pairs), False, col_scale)
        summed = jnp.sum(row_sum[...].reshape(-1, 8, pairs), axis=1)
        summed = spread(summed, True, row_scale)
        for n in range(vec_count):
            out_ref[n] = columns[n * point_local : (n + 1) * point_local]
            out_ref[vec_count + n] = summed[n * row_count : (n + 1) * row_count]
            low = (vec_count + n) * point_local
            out_ref[2 * vec_count + n] = columns[low : low + point_local]

    assert point_local == row_count
    return pl.pallas_call(
        kernel,
        out_shape=jax.ShapeDtypeStruct((3 * vec_count, row_count, pairs), jnp.float32),
        in_specs=[HBM] + [HBM, HBM, SMEM] * SIDES + [HBM] * (SIDES + 1),
        out_specs=VMEM,
        scratch_shapes=[
            pltpu.VMEM((most, depth, WIDE_ONE), jnp.bfloat16),
            pltpu.VMEM((most, pairs, depth), jnp.bfloat16),
            pltpu.VMEM((most, width, pairs), jnp.bfloat16),
            pltpu.VMEM((SIDES,) + vecs[0].shape, jnp.float32),
            pltpu.VMEM(row_vec.shape, jnp.float32),
            pltpu.VMEM((pairs, pairs), jnp.float32),
            pltpu.VMEM((pairs, pairs), jnp.float32),
            pltpu.VMEM((vec_count, row_count, 16, 8, pairs), jnp.float32),
            pltpu.VMEM((SIDES, vec_count, point_local, 16, pairs), jnp.float32),
        ]
        + [pltpu.SemaphoreType.DMA((most,))] * 4
        + [pltpu.SemaphoreType.DMA((SIDES + 1,))],
        compiler_params=pltpu.CompilerParams(vmem_limit_bytes=LIMIT),
        name="images",
    )(incoming, *sides[0], *sides[1], *vecs, row_vec)


def swap(values, axis, step):
    perm = [(i, i ^ step) for i in range(lax.axis_size(axis))]
    return lax.ppermute(values, axis, perm)


def on_device(row_orbitals, orbitals, screening, pair_blocks, row_vectors, vectors):
    ka_count = lax.axis_size("ka")
    ga_count = lax.axis_size("ga")
    half = ka_count // SIDES
    row_count = row_orbitals.shape[0]
    point_local, bands, grid = orbitals.shape
    block_local, wave_count, slice_width = screening.shape
    vec_count = vectors.shape[0]

    kind = lax.axis_index("ga") % 2
    part = lax.dynamic_slice_in_dim(orbitals, kind * NV, NV, 1)
    part = part.reshape(point_local * NV, grid)
    flat = lambda values: values.reshape(-1, NV * NC)
    beside = jnp.pad(flat(vectors), ((0, point_local * (NV - vec_count)), (0, 0)))
    fetched = swap(jnp.concatenate([part, beside], axis=1), "ka", half)

    table = pair_blocks.T
    outgoing = gather_blocks(table, jnp.swapaxes(screening, 1, 2), ka_count)
    outgoing, table = lax.optimization_barrier((outgoing, table))
    groups = [list(range(half)), list(range(half, ka_count))]
    incoming = lax.all_to_all(
        outgoing, "ka", split_axis=0, concat_axis=0, tiled=True, axis_index_groups=groups
    )

    rows = row_orbitals.reshape(row_count * bands, grid)
    sizes = (ka_count, block_local, slice_width, wave_count, vec_count * point_local)
    own, (own_vec, row_vec), plane = densities(
        0,
        table,
        (rows,),
        (orbitals.reshape(point_local * bands, grid),),
        (),
        (flat(vectors), flat(row_vectors)),
        sizes,
    )
    fetched, own_vec = lax.optimization_barrier((fetched, own_vec))
    passed = swap(fetched, "ga", 1)
    mirrored, (mirror_vec,), _ = densities(
        1, table, (), (fetched, passed), plane, (), sizes
    )
    row_scale = float(wave_count * NV * NC * point_local * ka_count) ** (-0.5)
    col_scale = float(wave_count * NV * NC * row_count) ** (-0.5)
    part = images(
        incoming,
        (own, mirrored),
        (own_vec, mirror_vec),
        row_vec,
        (vec_count, row_count, point_local),
        row_scale,
        col_scale,
        wave_count,
    )
    step = 1
    while step < ga_count:
        part = part + swap(part, "ga", step)
        step *= 2
    column = part[:vec_count]
    row = part[vec_count:]
    other = swap(row, "ka", half)
    row = row[:vec_count] + other[:vec_count]
    other, row = lax.optimization_barrier((other, row))
    column = column + other[vec_count:]
    step = 1
    while step < half:
        row = row + swap(row, "ka", step)
        step *= 2
    return row, column


def solution(mesh):
    return jax.shard_map(
        on_device,
        mesh=mesh,
        in_specs=(P(), P("ka", None, None), P("ka", None, "ga"), P(), P(), P(None, "ka", None)),
        out_specs=(P(), P(None, "ka", None)),
        check_vma=False,
    )
```

```python
import math

import jax
import jax.numpy as jnp
from jax import lax
from jax.experimental import pallas as pl
from jax.experimental.pallas import tpu as pltpu
from jax.sharding import PartitionSpec as P

NV = 16
NC = 16
CAP = 2
SIDES = 2
MAIN = 256
HALF = 64
WIDE = CAP * MAIN + 2 * HALF
WIDE_ONE = MAIN + 2 * HALF
AHEAD = 8
GROUP = 2
SPLIT = 3
LIMIT = 62 << 20
TAIL = 128
CHUNK = 512
NT = (((1,), (1,)), ((), ()))
VMEM = pl.BlockSpec(memory_space=pltpu.VMEM)
SMEM = pl.BlockSpec(memory_space=pltpu.SMEM)
HBM = pl.BlockSpec(memory_space=pltpu.HBM)


def mirror_of(device, count):
    half = count // SIDES
    return jnp.where(device < half, device + half, device - half)


def gather_blocks(table, blocks, ka_count):
    row_count = table.shape[0]
    point_local = table.shape[1] // ka_count
    block_local, depth, waves = blocks.shape
    rest = waves - MAIN
    half = ka_count // SIDES
    slots = half * SIDES

    def kernel(
        table_hbm, blocks_ref, out_ref, table_ref, held, shared, count, table_sem, in_sem, main_sem,
        shared_sem,
    ):
        me = lax.axis_index("ka")
        base = me * block_local
        first = jnp.where(me < half, 0, half)
        copy = pltpu.make_async_copy(table_hbm, table_ref, table_sem)
        copy.start()
        copy.wait()

        def block_copy(local, d, s):
            at = d * CAP + s
            return pltpu.make_async_copy(blocks_ref.at[local], held.at[at], in_sem.at[at])

        def main_copy(d, s):
            return pltpu.make_async_copy(
                held.at[d * CAP + s, :, pl.ds(0, MAIN)],
                out_ref.at[lax.rem(d, half), d // half, :, pl.ds(s * MAIN, MAIN)],
                main_sem.at[d * CAP + s],
            )

        def shared_copy(d):
            return pltpu.make_async_copy(
                shared.at[d],
                out_ref.at[lax.rem(d, half), d // half, :, pl.ds(CAP * MAIN, 2 * HALF)],
                shared_sem.at[d],
            )

        def start(d, carry):
            device = first + lax.rem(d, half)
            device = jnp.where(d < half, device, mirror_of(device, ka_count))
            taken = jnp.int32(0)
            for b in range(point_local):
                for a in range(row_count):
                    local = table_ref[a, device * point_local + b] - base
                    hit = (local >= 0) & (local < block_local) & (taken < CAP)

                    @pl.when(hit)
                    def _():
                        block_copy(local, d, taken).start()

                    taken = taken + hit.astype(jnp.int32)
            count[d] = taken
            return carry

        lax.fori_loop(0, slots, start, 0)

        def pack(d, carry):
            for s in range(CAP):

                @pl.when(count[d] > s)
                def _():
                    block_copy(0, d, s).wait()
                    main_copy(d, s).start()
                    shared[d, :, s * HALF : s * HALF + rest] = held[d * CAP + s, :, MAIN:]

            @pl.when(count[d] > 0)
            def _():
                shared_copy(d).start()

            return carry

        lax.fori_loop(0, slots, pack, 0)

        def finish(d, carry):
            for s in range(CAP):

                @pl.when(count[d] > s)
                def _():
                    main_copy(d, s).wait()

            @pl.when(count[d] > 0)
            def _():
                shared_copy(d).wait()

            return carry

        lax.fori_loop(0, slots, finish, 0)

    return pl.pallas_call(
        kernel,
        out_shape=jax.ShapeDtypeStruct((half, SIDES, depth, WIDE), jnp.bfloat16),
        in_specs=[HBM, HBM],
        out_specs=HBM,
        scratch_shapes=[
            pltpu.SMEM(table.shape, jnp.int32),
            pltpu.VMEM((slots * CAP, depth, waves), jnp.bfloat16),
            pltpu.VMEM((slots, depth, 2 * HALF), jnp.bfloat16),
            pltpu.SMEM((slots,), jnp.int32),
            pltpu.SemaphoreType.DMA,
            pltpu.SemaphoreType.DMA((slots * CAP,)),
            pltpu.SemaphoreType.DMA((slots * CAP,)),
            pltpu.SemaphoreType.DMA((slots,)),
        ],
        compiler_params=pltpu.CompilerParams(vmem_limit_bytes=LIMIT),
        name="gather_blocks",
    )(table, blocks)


def spread_vectors(vec_ref, keep_second, order):
    count, pairs = len(order), vec_ref.shape[1]
    row = lax.broadcasted_iota(jnp.int32, (count * 16, pairs), 0)
    lane = lax.broadcasted_iota(jnp.int32, (count * 16, pairs), 1)
    values = vec_ref[...].astype(jnp.float32)
    values = jnp.concatenate(
        [jnp.broadcast_to(values[i : i + 1], (16, pairs)) for i in order], axis=0
    )
    values = jnp.where(lane // 16 == row % 16, values, 0.0).astype(jnp.bfloat16)
    at = lax.broadcasted_iota(jnp.int32, (pairs, pairs), 0)
    to = lax.broadcasted_iota(jnp.int32, (pairs, pairs), 1)
    index = to % 16 if keep_second else to // 16
    pick = jnp.where(at % 16 == index, 1.0, 0.0).astype(jnp.bfloat16)
    return jnp.dot(values, pick, preferred_element_type=jnp.float32).reshape(count, 16, pairs)


def densities(side, table, rows, pieces, plane, vecs, sizes, begun=()):
    ka_count, block_local, depth, waves, vec_rows, grid = sizes
    row_count = table.shape[0]
    point_local = table.shape[1] // ka_count
    pair_count = row_count * point_local
    quarter = grid // 4
    segment = quarter + TAIL
    points = segment + quarter
    width = WIDE_ONE
    evens, odds = (waves + 1) // 2, waves // 2
    half = ka_count // SIDES
    pairs = NV * NV
    block = 256
    n_piece = len(pieces)
    n_vec = len(vecs) + side
    make_plane = not plane
    resume = bool(begun)

    def cosine(phase):
        phase = phase & (grid - 1) if grid & (grid - 1) == 0 else jnp.remainder(phase, grid)
        away = jnp.abs(phase - grid // 2)
        z = 1.0 - away.astype(jnp.float32) * (4.0 / grid)
        square = z * z
        value = jnp.zeros_like(z)
        for k in (11, 9, 7, 5, 3, 1):
            term = (math.pi / 2) ** k / math.factorial(k) * (-1.0) ** (k // 2)
            value = value * square + term
        return value * -z

    def waves_of(shape):
        lane = lax.broadcasted_iota(jnp.int32, shape, 1)
        parity = (lane >= 2 * MAIN).astype(jnp.int32)
        column = lane - MAIN - parity * MAIN
        wave = jnp.where(
            lane < MAIN, lane + lax.axis_index("ga") * depth, 2 * column + parity
        )
        return wave, (lane < depth) | ((lane >= MAIN) & (column >= 0) & (wave < waves))

    def kernel(*refs):
        refs = list(refs)
        take = lambda count: [refs.pop(0) for _ in range(count)]
        (table_hbm,) = take(1)
        row_hbm = take(1)[0] if make_plane else None
        piece_hbm = take(n_piece)
        plane_in = take(len(plane))
        vec_refs = take(len(vecs))
        list_in = take(len(begun))[2:]
        vale_ref, cond_ref = take(2)
        (list_ref,) = list_in or take(1)
        vec_out = take(n_vec)
        plane_out = take(5 if make_plane else 0)
        table_ref, ket_raw, vplane, eplane, oplane = take(5)
        row_raw, cos_part, sin_part = take(3 if make_plane else 0) or (None,) * 3
        vec_raw = take(1)[0] if side else None
        bras, kets, fv, fe, fo, natural, vbuf, cbuf, seen = take(9)
        load_sem, out_sem, plane_sem = take(3)

        me = lax.axis_index("ka")
        source = me if side == 0 else mirror_of(me, ka_count)
        first = jnp.where(me < half, 0, half)

        loads = [pltpu.make_async_copy(table_hbm, table_ref, load_sem.at[0])]
        if make_plane:
            loads.append(pltpu.make_async_copy(row_hbm, row_raw, load_sem.at[1]))
        ready = len(loads)
        low = 0
        for i, ref in enumerate(piece_hbm):
            size = ref.shape[0]
            loads.append(
                pltpu.make_async_copy(
                    ref.at[:, pl.ds(0, grid)], ket_raw.at[pl.ds(low, size)], load_sem.at[2 + i]
                )
            )
            low += size
        for i, (ref, to) in enumerate(zip(plane_in, (vplane, eplane, oplane, bras, kets))):
            loads.append(pltpu.make_async_copy(ref, to, load_sem.at[4 + i]))
        if side:
            loads.append(
                pltpu.make_async_copy(
                    piece_hbm[0].at[:, pl.ds(grid, pairs)],
                    vec_raw,
                    load_sem.at[9],
                )
            )
            vec_refs = [vec_raw]
            vec_count = vec_rows // point_local
            orders = [[n * 16 + b for n in range(vec_count) for b in range(point_local)]]
        else:
            orders = [range(vec_rows)] * n_vec
        for load in loads:
            load.start()

        if make_plane:
            wave, valid = waves_of(cos_part.shape)
            point = lax.broadcasted_iota(jnp.int32, cos_part.shape, 0)
            scale = jnp.where(valid, math.sqrt(2.0 / grid), 0.0)
            cos_part[...] = cosine(wave * point) * scale
            sin_part[...] = cosine(wave * point - grid // 4) * scale
            wave8, _ = waves_of((8, cos_part.shape[1]))

            def fill(step, carry):
                at = pl.ds(pl.multiple_of(step * TAIL, TAIL), TAIL)
                turn = wave8 * (step * TAIL)
                value = cosine(turn)[:1] * cos_part[...]
                value -= cosine(turn - grid // 4)[:1] * sin_part[...]
                value = value.astype(jnp.bfloat16)
                vplane[at, :] = value[:, :depth]
                eplane[at, :] = value[:, MAIN : MAIN + evens]
                oplane[at, :] = value[:, 2 * MAIN : 2 * MAIN + odds]
                return carry

            def fill_back(step, carry):
                at = pl.ds(pl.multiple_of(segment + step * TAIL, TAIL), TAIL)
                turn = wave8[:, :MAIN] * (grid // 2 - step * TAIL)
                value = cosine(turn)[:1] * cos_part[:, :MAIN]
                value += cosine(turn - grid // 4)[:1] * sin_part[:, :MAIN]
                vplane[at, :] = value.astype(jnp.bfloat16)[:, :depth]
                return carry

            lax.fori_loop(0, segment // TAIL, fill, 0)
            lax.fori_loop(0, quarter // TAIL, fill_back, 0)

        at = lax.broadcasted_iota(jnp.int32, (2 * block, block), 0)
        to = lax.broadcasted_iota(jnp.int32, (2 * block, block), 1)
        flip = ((at < block) & (at + to == block)) | ((at == block) & (to == 0))
        flip = jnp.where(flip, 1.0, 0.0).astype(jnp.bfloat16)

        def fold(src, low, size, put):
            rows_at = slice(low, low + size)
            lane = lax.broadcasted_iota(jnp.int32, (size, block), 1)

            def turned(begin, end):
                return jnp.dot(
                    src[rows_at, begin:end], flip[: end - begin], preferred_element_type=jnp.float32
                )

            for at in range(0, quarter, block):
                end = grid - at - block
                there = src[rows_at, grid // 2 + at : grid // 2 + at + block].astype(jnp.float32)
                parts = (
                    src[rows_at, at : at + block].astype(jnp.float32),
                    turned(end, min(end + 2 * block, grid)),
                    turned(end - grid // 2, end - grid // 2 + 2 * block),
                    there if at else jnp.where(lane == 0, 0.0, there),
                )
                for k, values in enumerate(parts):
                    put(slice(k * segment + at, k * segment + at + block), values)
            for k in range(2):
                at = (2 * k + 1) * quarter
                last = src[rows_at, at : at + TAIL].astype(jnp.float32)
                at = k * segment + quarter
                put(slice(at, at + TAIL), jnp.where(lane[:, :TAIL] == 0, last, 0.0))

        def put_whole(ref):
            def put(lanes, values):
                ref[:, :, :, lanes] = values.reshape(-1, 2, 16, values.shape[1])

            return put

        def put_part(ref, kind):
            def put(lanes, values):
                for b in range(point_local):
                    ref[b, kind, :, lanes] = values[b * 16 : (b + 1) * 16]

            return put

        stores = []
        if make_plane:
            loads[1].wait()
            fold(row_raw, 0, row_raw.shape[0], put_whole(bras))
            stores = [
                pltpu.make_async_copy(ref, to, plane_sem.at[i])
                for i, (ref, to) in enumerate(zip((vplane, eplane, oplane, bras, kets), plane_out))
            ]
            for store in stores[:4]:
                store.start()
        for i in range(n_piece):
            loads[ready + i].wait()
        if n_piece == 1:
            fold(ket_raw, 0, ket_raw.shape[0], put_whole(kets))
            stores[4].start()
        elif n_piece:
            kind = lax.axis_index("ga") % 2
            size = point_local * 16
            fold(ket_raw, 0, size, put_part(kets, kind))
            fold(ket_raw, size, size, put_part(kets, 1 - kind))
        for load in loads[:1] + loads[ready + n_piece :]:
            load.wait()
        for i in range(n_vec):
            vec_out[i][...] = spread_vectors(vec_refs[i], i == 0, orders[i])

        def listed(p, carry):
            b = p // row_count
            a = lax.rem(p, row_count)
            owner = table_ref[a, source * point_local + b] // block_local - first

            @pl.when((owner >= 0) & (owner < half))
            def _():
                at = list_ref[0]
                list_ref[1 + 3 * at] = p
                list_ref[2 + 3 * at] = owner
                list_ref[3 + 3 * at] = seen[owner]
                list_ref[0] = at + 1
                seen[owner] = seen[owner] + 1

            return carry

        if not resume:
            for t in range(half):
                seen[t] = 0
            for f in range(4):
                list_ref[f] = 0
            lax.fori_loop(0, pair_count, listed, 0)
        count = list_ref[0]
        trips = (count + GROUP - 1) // GROUP
        begin = jnp.minimum(SPLIT, trips) if resume else 0
        end = jnp.minimum(SPLIT, trips) if make_plane else trips

        def outputs(n, g):
            slot = lax.rem(n, 2)
            p = list_ref[1 + 3 * jnp.minimum(n * GROUP + g, pair_count - 1)]
            return (
                pltpu.make_async_copy(vbuf.at[slot, g], vale_ref.at[p], out_sem.at[slot, g, 0]),
                pltpu.make_async_copy(cbuf.at[slot, g], cond_ref.at[p], out_sem.at[slot, g, 1]),
            )

        def finish(n):
            for g in range(GROUP):

                @pl.when((n >= begin) & (n * GROUP + g < count))
                def _():
                    for copy in outputs(n, g):
                        copy.wait()

        def group(n, carry):
            finish(n - 2)
            slot = lax.rem(n, 2)
            entries = [list_ref[1 + 3 * jnp.minimum(n * GROUP + g, count - 1)] for g in range(GROUP)]
            places = [(lax.rem(p, row_count), p // row_count) for p in entries]

            def products(kind, t):
                spans = range(4 if t < quarter else 2)
                lanes = [slice(k * segment + t, k * segment + t + 128) for k in spans]
                for g, (a, b) in enumerate(places):
                    ket = [kets[b, kind, :, at] for at in lanes]
                    for c in range(16):
                        bra = [bras[a, kind, c : c + 1, at] for at in lanes]
                        row = g * pairs + c * 16
                        yield slice(row, row + 16), [
                            bra[k] * ket[k] + bra[k + 1] * ket[k + 1] for k in spans[::2]
                        ]

            def times(lhs, low, high, plane_ref, total):
                part = jnp.dot(
                    lhs[:, low:high], plane_ref[low:high, :], preferred_element_type=jnp.float32
                )
                return part if total is None else total + part

            sums = {"vale": None, "even": None, "odd": None}

            def cond_products(low, high):
                for t in range(low, high, 128):
                    for at, value in products(1, t):
                        if t < quarter:
                            fe[at, t : t + 128] = (value[0] + value[1]).astype(jnp.bfloat16)
                            fo[at, t : t + 128] = (value[0] - value[1]).astype(jnp.bfloat16)
                        else:
                            fe[at, t : t + 128] = value[0].astype(jnp.bfloat16)

            def cond_sums(low, high):
                sums["even"] = times(fe, low, high, eplane, sums["even"])
                if low < quarter:
                    sums["odd"] = times(fo, low, high, oplane, sums["odd"])

            def vale_products(low, high):
                for t in range(low, high, 128):
                    for at, value in products(0, t):
                        for k, part in enumerate(value):
                            to = k * segment + t
                            fv[at, to : to + 128] = part.astype(jnp.bfloat16)

            def vale_sums(low, high):
                sums["vale"] = times(fv, low, high, vplane, sums["vale"])
                if low < quarter:
                    sums["vale"] = times(fv, segment + low, segment + high, vplane, sums["vale"])

            def cond_out():
                rest = waves - MAIN
                blank = jnp.zeros((HALF - rest, pairs), jnp.bfloat16)
                for g in range(GROUP):
                    for h in range(pairs // 128):
                        rows_at = slice(g * pairs + h * 128, g * pairs + (h + 1) * 128)
                        lanes = slice(h * 128, (h + 1) * 128)
                        natural[h, pl.ds(0, evens, stride=2), :] = sums["even"][rows_at].T
                        natural[h, pl.ds(1, odds, stride=2), :] = sums["odd"][rows_at].T
                        cbuf[slot, g, :waves, lanes] = natural[h, :waves].astype(jnp.bfloat16)
                        cbuf[slot, g, MAIN + HALF : waves + HALF, lanes] = natural[
                            h, MAIN:waves
                        ].astype(jnp.bfloat16)
                    cbuf[slot, g, waves : MAIN + HALF] = blank
                    cbuf[slot, g, waves + HALF :] = blank

            chunks = [(low, min(low + CHUNK, segment)) for low in range(0, segment, CHUNK)]
            steps = [(cond_products, cond_sums, chunk) for chunk in chunks]
            steps += [(vale_products, vale_sums, chunk) for chunk in chunks]
            steps[0][0](*steps[0][2])
            for at, (_, add, chunk) in enumerate(steps):
                if at + 1 < len(steps):
                    steps[at + 1][0](*steps[at + 1][2])
                add(*chunk)
                if at == len(chunks):
                    cond_out()
            vbuf[slot] = sums["vale"].astype(jnp.bfloat16).reshape(GROUP, pairs, depth)
            for g in range(GROUP):

                @pl.when(n * GROUP + g < count)
                def _():
                    for copy in outputs(n, g):
                        copy.start()

            return carry

        lax.fori_loop(begin, end, group, 0)
        finish(end - 2)
        finish(end - 1)
        for store in stores:
            store.wait()

    folded = lambda count: pltpu.VMEM((count, 2, 16, 4 * segment), jnp.float32)
    plane_shapes = [
        jax.ShapeDtypeStruct((points, depth), jnp.bfloat16),
        jax.ShapeDtypeStruct((segment, evens), jnp.bfloat16),
        jax.ShapeDtypeStruct((segment, odds), jnp.bfloat16),
        jax.ShapeDtypeStruct((row_count, 2, 16, 4 * segment), jnp.float32),
        jax.ShapeDtypeStruct((point_local, 2, 16, 4 * segment), jnp.float32),
    ]
    n_in = 1 + len(rows) + n_piece + len(plane)
    n_list = 0 if resume else 1
    result = pl.pallas_call(
        kernel,
        out_shape=[
            jax.ShapeDtypeStruct((pair_count, pairs, depth), jnp.bfloat16),
            jax.ShapeDtypeStruct((pair_count, width, pairs), jnp.bfloat16),
        ]
        + [jax.ShapeDtypeStruct((1 + 3 * pair_count,), jnp.int32)] * n_list
        + [jax.ShapeDtypeStruct((vec_rows, 16, pairs), jnp.float32)] * n_vec
        + (plane_shapes if make_plane else []),
        in_specs=[HBM] * n_in + [VMEM] * len(vecs) + ([HBM, HBM, SMEM] if resume else []),
        out_specs=[HBM, HBM]
        + [SMEM] * n_list
        + [VMEM] * n_vec
        + ([HBM] * len(plane_shapes) if make_plane else []),
        input_output_aliases={n_in: 0, n_in + 1: 1} if resume else {},
        scratch_shapes=[
            pltpu.SMEM(table.shape, jnp.int32),
            pltpu.VMEM((point_local * 32, grid), jnp.bfloat16),
            pltpu.VMEM((points, depth), jnp.bfloat16),
            pltpu.VMEM((segment, evens), jnp.bfloat16),
            pltpu.VMEM((segment, odds), jnp.bfloat16),
        ]
        + (
            [
                pltpu.VMEM(rows[0].shape, jnp.bfloat16),
                pltpu.VMEM((TAIL, 3 * MAIN), jnp.float32),
                pltpu.VMEM((TAIL, 3 * MAIN), jnp.float32),
            ]
            if make_plane
            else [pltpu.VMEM((point_local * 16, pairs), jnp.bfloat16)] * side
        )
        + [
            folded(row_count),
            folded(point_local),
            pltpu.VMEM((GROUP * pairs, points), jnp.bfloat16),
            pltpu.VMEM((GROUP * pairs, segment), jnp.bfloat16),
            pltpu.VMEM((GROUP * pairs, quarter), jnp.bfloat16),
            pltpu.VMEM((pairs // 128, 2 * evens, 128), jnp.float32),
            pltpu.VMEM((2, GROUP, pairs, depth), jnp.bfloat16),
            pltpu.VMEM((2, GROUP, width, pairs), jnp.bfloat16),
            pltpu.SMEM((half,), jnp.int32),
            pltpu.SemaphoreType.DMA((10,)),
            pltpu.SemaphoreType.DMA((2, GROUP, 2)),
            pltpu.SemaphoreType.DMA((5,)),
        ],
        compiler_params=pltpu.CompilerParams(vmem_limit_bytes=LIMIT),
        cost_estimate=pl.CostEstimate(
            flops=5 * 10**10 if side else 1, bytes_accessed=10**6, transcendentals=0
        ),
        name="densities_mirror" if side else "densities_rest" if resume else "densities_own",
    )(table, *rows, *pieces, *plane, *vecs, *begun)
    if resume:
        return (*result, begun[2])
    return result[:3], result[3 : 3 + n_vec], result[3 + n_vec :]


def images(incoming, sides, vecs, row_vec, counts, row_scale, col_scale, wave_count):
    pair_count, pairs, depth = sides[0][0].shape
    width = sides[0][1].shape[1]
    vec_count, row_count, point_local = counts
    rest = wave_count - MAIN
    most = SIDES * pair_count

    def kernel(*refs):
        refs = list(refs)
        take = lambda count: [refs.pop(0) for _ in range(count)]
        (block_ref,) = take(1)
        side_refs = [take(3) for _ in range(SIDES)]
        vec_hbm = take(SIDES)
        rowvec_hbm, out_ref = take(2)
        block_buf, vale_buf, cond_buf, vec_buf, rowvec_ref, ready, even, odd, row_sum, col_sum = take(10)
        main_sem, shared_sem, vale_sem, cond_sem, vec_sem = take(5)

        own_count = side_refs[0][2][0]
        count = own_count + side_refs[1][2][0]

        def field(i, f):
            i = jnp.clip(i, 0, count - 1)
            own = side_refs[0][2][1 + 3 * jnp.minimum(i, pair_count - 1) + f]
            other = side_refs[1][2][1 + 3 * jnp.maximum(i - own_count, 0) + f]
            return jnp.where(i < own_count, own, other)

        def copies(k, i):
            vale_ref, cond_ref, _ = side_refs[k]
            p, owner, rank = (field(i, f) for f in range(3))
            lanes = pl.ds(pl.multiple_of(rank * MAIN, MAIN), MAIN)
            return (
                pltpu.make_async_copy(vale_ref.at[p], vale_buf.at[i], vale_sem.at[i]),
                pltpu.make_async_copy(
                    block_ref.at[owner, k, :, lanes],
                    block_buf.at[i, :, pl.ds(0, MAIN)],
                    main_sem.at[i],
                ),
                pltpu.make_async_copy(
                    block_ref.at[owner, k, :, pl.ds(CAP * MAIN, 2 * HALF)],
                    block_buf.at[i, :, pl.ds(MAIN, 2 * HALF)],
                    shared_sem.at[i],
                ),
                pltpu.make_async_copy(cond_ref.at[p], cond_buf.at[i], cond_sem.at[i]),
            )

        def start(i):
            for k in range(SIDES):
                low = own_count if k else 0
                high = count if k else own_count

                @pl.when((i >= low) & (i < high))
                def _():
                    for copy in copies(k, i):
                        copy.start()

        def arrived(i):
            for copy in copies(0, i):
                copy.wait()

        for i in range(AHEAD):
            start(i)
        vec_copies = [
            pltpu.make_async_copy(ref, to, vec_sem.at[k])
            for k, (ref, to) in enumerate(
                [(rowvec_hbm, rowvec_ref)] + [(vec_hbm[k], vec_buf.at[k]) for k in range(SIDES)]
            )
        ]
        for copy in vec_copies:
            copy.start()
        row_sum[...] = jnp.zeros(row_sum.shape, jnp.float32)
        col_sum[...] = jnp.zeros(col_sum.shape, jnp.float32)
        odd[...] = jnp.zeros(odd.shape, jnp.float32)
        for copy in vec_copies:
            copy.wait()

        def screen(i):
            at = jnp.minimum(i, count - 1)
            lane = lax.broadcasted_iota(jnp.int32, (depth, 2 * HALF), 1)
            begin = field(i, 2) * HALF
            mine = (lane >= begin) & (lane < begin + rest)
            shared = jnp.where(mine, block_buf[at, :, MAIN:].astype(jnp.float32), 0.0)
            block = jnp.concatenate([block_buf[at, :, :MAIN], shared.astype(jnp.bfloat16)], axis=1)
            return jnp.dot(block, cond_buf[at], preferred_element_type=jnp.float32).astype(
                jnp.bfloat16
            )

        def multiply(i, screened, into):
            at = jnp.minimum(i, count - 1)
            matrix = jnp.dot(vale_buf[at], screened, preferred_element_type=jnp.float32)
            into[...] = jnp.where(i < count, matrix, 0.0)

        def contract(i, matrix):
            p = field(i, 0)
            k = (jnp.clip(i, 0, count - 1) >= own_count).astype(jnp.int32)
            b = p // row_count
            a = lax.rem(p, row_count)
            totals = [jnp.zeros((16, pairs), jnp.float32)] * vec_count
            ket = [vec_buf[k, n * point_local + b] for n in range(vec_count)]
            for v in range(16):
                part = matrix[v * 16 : (v + 1) * 16, :]
                for n in range(vec_count):
                    term = part * ket[n]
                    row_sum[n, a, v] += term[:8] + term[8:]
                    totals[n] += part * rowvec_ref[n * row_count + a, v : v + 1, :]
            for n in range(vec_count):
                col_sum[k, n, b] += totals[n]

        def arrive(i):
            @pl.when(i < count)
            def _():
                arrived(i)

        @pl.when(count > 0)
        def _():
            for i in range(2):
                arrive(i)
            for i in range(2):
                ready[i] = screen(i)

        def two(j, carry):
            for i in range(2):
                start(2 * j + AHEAD + i)
            for i in range(2):
                arrive(2 * j + 2 + i)
            multiply(2 * j, ready[0], even)
            first = screen(2 * j + 2)
            contract(2 * j - 1, odd)
            multiply(2 * j + 1, ready[1], odd)
            second = screen(2 * j + 3)
            contract(2 * j, even)
            ready[0] = first
            ready[1] = second
            return carry

        trips = (count + 1) // 2
        lax.fori_loop(0, trips, two, 0)

        @pl.when(count > 0)
        def _():
            contract(2 * trips - 1, odd)

        def spread(values, keep_first, scale):
            at = lax.broadcasted_iota(jnp.int32, (pairs, pairs), 0)
            to = lax.broadcasted_iota(jnp.int32, (pairs, pairs), 1)
            index = at // 16 if keep_first else at % 16
            pick = jnp.where(index == to % 16, 1.0, 0.0).astype(jnp.bfloat16)
            high = values.astype(jnp.bfloat16)
            low = (values - high.astype(jnp.float32)).astype(jnp.bfloat16)
            wide = jnp.dot(high, pick, preferred_element_type=jnp.float32) + jnp.dot(
                low, pick, preferred_element_type=jnp.float32
            )
            row = lax.broadcasted_iota(jnp.int32, wide.shape, 0)
            lane = lax.broadcasted_iota(jnp.int32, wide.shape, 1)
            wide = jnp.where(row % 16 == lane // 16, wide, 0.0)
            return jnp.sum(wide.reshape(-1, 16, pairs), axis=1) * scale

        columns = spread(col_sum[...].reshape(-1, pairs), False, col_scale)
        summed = jnp.sum(row_sum[...].reshape(-1, 8, pairs), axis=1)
        summed = spread(summed, True, row_scale)
        for n in range(vec_count):
            out_ref[n] = columns[n * point_local : (n + 1) * point_local]
            out_ref[vec_count + n] = summed[n * row_count : (n + 1) * row_count]
            low = (vec_count + n) * point_local
            out_ref[2 * vec_count + n] = columns[low : low + point_local]

    assert point_local == row_count
    return pl.pallas_call(
        kernel,
        out_shape=jax.ShapeDtypeStruct((3 * vec_count, row_count, pairs), jnp.float32),
        in_specs=[HBM] + [HBM, HBM, SMEM] * SIDES + [HBM] * (SIDES + 1),
        out_specs=VMEM,
        scratch_shapes=[
            pltpu.VMEM((most, depth, WIDE_ONE), jnp.bfloat16),
            pltpu.VMEM((most, pairs, depth), jnp.bfloat16),
            pltpu.VMEM((most, width, pairs), jnp.bfloat16),
            pltpu.VMEM((SIDES,) + vecs[0].shape, jnp.float32),
            pltpu.VMEM(row_vec.shape, jnp.float32),
            pltpu.VMEM((2, depth, pairs), jnp.bfloat16),
            pltpu.VMEM((pairs, pairs), jnp.float32),
            pltpu.VMEM((pairs, pairs), jnp.float32),
            pltpu.VMEM((vec_count, row_count, 16, 8, pairs), jnp.float32),
            pltpu.VMEM((SIDES, vec_count, point_local, 16, pairs), jnp.float32),
        ]
        + [pltpu.SemaphoreType.DMA((most,))] * 4
        + [pltpu.SemaphoreType.DMA((SIDES + 1,))],
        compiler_params=pltpu.CompilerParams(vmem_limit_bytes=LIMIT),
        name="images",
    )(incoming, *sides[0], *sides[1], *vecs, row_vec)


def swap(values, axis, step):
    perm = [(i, i ^ step) for i in range(lax.axis_size(axis))]
    return lax.ppermute(values, axis, perm)


def on_device(row_orbitals, orbitals, screening, pair_blocks, row_vectors, vectors):
    ka_count = lax.axis_size("ka")
    ga_count = lax.axis_size("ga")
    half = ka_count // SIDES
    row_count = row_orbitals.shape[0]
    point_local, bands, grid = orbitals.shape
    block_local, wave_count, slice_width = screening.shape
    vec_count = vectors.shape[0]

    kind = lax.axis_index("ga") % 2
    part = lax.dynamic_slice_in_dim(orbitals, kind * NV, NV, 1)
    assert vec_count == point_local
    flat = lambda values: values.reshape(-1, NV * NC)
    beside = jnp.pad(vectors, ((0, 0), (0, NV - point_local), (0, 0)))
    part = jnp.concatenate([part, beside], axis=2).reshape(point_local * NV, -1)
    fetched = swap(part, "ka", half)

    table = pair_blocks.T
    outgoing = gather_blocks(table, jnp.swapaxes(screening, 1, 2), ka_count)
    outgoing, table = lax.optimization_barrier((outgoing, table))
    groups = [list(range(half)), list(range(half, ka_count))]
    incoming = lax.all_to_all(
        outgoing, "ka", split_axis=0, concat_axis=0, tiled=True, axis_index_groups=groups
    )

    rows = row_orbitals.reshape(row_count * bands, grid)
    sizes = (ka_count, block_local, slice_width, wave_count, vec_count * point_local, grid)
    own, (own_vec, row_vec), plane = densities(
        0,
        table,
        (rows,),
        (orbitals.reshape(point_local * bands, grid),),
        (),
        (flat(vectors), flat(row_vectors)),
        sizes,
    )
    fetched, own = lax.optimization_barrier((fetched, tuple(own)))
    passed = swap(fetched, "ga", 1)
    own = densities(0, table, (), (), plane, (), sizes, own)
    mirrored, (mirror_vec,), _ = densities(
        1, table, (), (fetched, passed), plane[:4], (), sizes
    )
    row_scale = float(wave_count * NV * NC * point_local * ka_count) ** (-0.5)
    col_scale = float(wave_count * NV * NC * row_count) ** (-0.5)
    part = images(
        incoming,
        (own, mirrored),
        (own_vec, mirror_vec),
        row_vec,
        (vec_count, row_count, point_local),
        row_scale,
        col_scale,
        wave_count,
    )
    step = 1
    while step < ga_count:
        part = part + swap(part, "ga", step)
        step *= 2
    column = part[:vec_count]
    row = part[vec_count:]
    other = swap(row, "ka", half)
    row = row[:vec_count] + other[:vec_count]
    other, row = lax.optimization_barrier((other, row))
    column = column + other[vec_count:]
    step = 1
    while step < half:
        row = row + swap(row, "ka", step)
        step *= 2
    return row, column


def solution(mesh):
    return jax.shard_map(
        on_device,
        mesh=mesh,
        in_specs=(P(), P("ka", None, None), P("ka", None, "ga"), P(), P(), P(None, "ka", None)),
        out_specs=(P(), P(None, "ka", None)),
        check_vma=False,
    )
```

```python
import math

import jax
import jax.numpy as jnp
from jax import lax
from jax.experimental import pallas as pl
from jax.experimental.pallas import tpu as pltpu
from jax.sharding import PartitionSpec as P

NV = 16
NC = 16
CAP = 2
SIDES = 2
MAIN = 256
HALF = 64
WIDE = CAP * MAIN + 2 * HALF
WIDE_ONE = MAIN + 2 * HALF
AHEAD = 8
GROUP = 2
SPLIT = 3
LIMIT = 62 << 20
WHOLE = (63 << 20) + (3 << 18)
TAIL = 128
CHUNK = 512
NT = (((1,), (1,)), ((), ()))
VMEM = pl.BlockSpec(memory_space=pltpu.VMEM)
SMEM = pl.BlockSpec(memory_space=pltpu.SMEM)
HBM = pl.BlockSpec(memory_space=pltpu.HBM)


def mirror_of(device, count):
    half = count // SIDES
    return jnp.where(device < half, device + half, device - half)


def gather_blocks(table, blocks, ka_count):
    row_count = table.shape[0]
    point_local = table.shape[1] // ka_count
    block_local, depth, waves = blocks.shape
    rest = waves - MAIN
    half = ka_count // SIDES
    slots = half * SIDES

    def kernel(
        table_hbm, blocks_ref, out_ref, table_ref, held, shared, count, table_sem, in_sem, main_sem,
        shared_sem,
    ):
        me = lax.axis_index("ka")
        base = me * block_local
        first = jnp.where(me < half, 0, half)
        copy = pltpu.make_async_copy(table_hbm, table_ref, table_sem)
        copy.start()
        copy.wait()

        def block_copy(local, d, s):
            at = d * CAP + s
            return pltpu.make_async_copy(blocks_ref.at[local], held.at[at], in_sem.at[at])

        def main_copy(d, s):
            return pltpu.make_async_copy(
                held.at[d * CAP + s, :, pl.ds(0, MAIN)],
                out_ref.at[lax.rem(d, half), d // half, :, pl.ds(s * MAIN, MAIN)],
                main_sem.at[d * CAP + s],
            )

        def shared_copy(d):
            return pltpu.make_async_copy(
                shared.at[d],
                out_ref.at[lax.rem(d, half), d // half, :, pl.ds(CAP * MAIN, 2 * HALF)],
                shared_sem.at[d],
            )

        def start(d, carry):
            device = first + lax.rem(d, half)
            device = jnp.where(d < half, device, mirror_of(device, ka_count))
            taken = jnp.int32(0)
            for b in range(point_local):
                for a in range(row_count):
                    local = table_ref[a, device * point_local + b] - base
                    hit = (local >= 0) & (local < block_local) & (taken < CAP)

                    @pl.when(hit)
                    def _():
                        block_copy(local, d, taken).start()

                    taken = taken + hit.astype(jnp.int32)
            count[d] = taken
            return carry

        lax.fori_loop(0, slots, start, 0)

        def pack(d, carry):
            for s in range(CAP):

                @pl.when(count[d] > s)
                def _():
                    block_copy(0, d, s).wait()
                    main_copy(d, s).start()
                    shared[d, :, s * HALF : s * HALF + rest] = held[d * CAP + s, :, MAIN:]

            @pl.when(count[d] > 0)
            def _():
                shared_copy(d).start()

            return carry

        lax.fori_loop(0, slots, pack, 0)

        def finish(d, carry):
            for s in range(CAP):

                @pl.when(count[d] > s)
                def _():
                    main_copy(d, s).wait()

            @pl.when(count[d] > 0)
            def _():
                shared_copy(d).wait()

            return carry

        lax.fori_loop(0, slots, finish, 0)

    return pl.pallas_call(
        kernel,
        out_shape=jax.ShapeDtypeStruct((half, SIDES, depth, WIDE), jnp.bfloat16),
        in_specs=[HBM, HBM],
        out_specs=HBM,
        scratch_shapes=[
            pltpu.SMEM(table.shape, jnp.int32),
            pltpu.VMEM((slots * CAP, depth, waves), jnp.bfloat16),
            pltpu.VMEM((slots, depth, 2 * HALF), jnp.bfloat16),
            pltpu.SMEM((slots,), jnp.int32),
            pltpu.SemaphoreType.DMA,
            pltpu.SemaphoreType.DMA((slots * CAP,)),
            pltpu.SemaphoreType.DMA((slots * CAP,)),
            pltpu.SemaphoreType.DMA((slots,)),
        ],
        compiler_params=pltpu.CompilerParams(vmem_limit_bytes=LIMIT),
        name="gather_blocks",
    )(table, blocks)


def spread_vectors(vec_ref, keep_second, order):
    count, pairs = len(order), vec_ref.shape[1]
    row = lax.broadcasted_iota(jnp.int32, (count * 16, pairs), 0)
    lane = lax.broadcasted_iota(jnp.int32, (count * 16, pairs), 1)
    values = vec_ref[...].astype(jnp.float32)
    values = jnp.concatenate(
        [jnp.broadcast_to(values[i : i + 1], (16, pairs)) for i in order], axis=0
    )
    values = jnp.where(lane // 16 == row % 16, values, 0.0).astype(jnp.bfloat16)
    at = lax.broadcasted_iota(jnp.int32, (pairs, pairs), 0)
    to = lax.broadcasted_iota(jnp.int32, (pairs, pairs), 1)
    index = to % 16 if keep_second else to // 16
    pick = jnp.where(at % 16 == index, 1.0, 0.0).astype(jnp.bfloat16)
    return jnp.dot(values, pick, preferred_element_type=jnp.float32).reshape(count, 16, pairs)


def densities(side, table, rows, pieces, plane, vecs, sizes, begun=()):
    ka_count, block_local, depth, waves, vec_rows, grid = sizes
    row_count = table.shape[0]
    point_local = table.shape[1] // ka_count
    pair_count = row_count * point_local
    quarter = grid // 4
    segment = quarter + TAIL
    points = segment + quarter
    width = WIDE_ONE
    evens, odds = (waves + 1) // 2, waves // 2
    half = ka_count // SIDES
    pairs = NV * NV
    block = 256
    n_piece = len(pieces)
    n_vec = len(vecs) + side
    make_plane = not plane
    resume = bool(begun)

    def cosine(phase):
        phase = phase & (grid - 1) if grid & (grid - 1) == 0 else jnp.remainder(phase, grid)
        away = jnp.abs(phase - grid // 2)
        z = 1.0 - away.astype(jnp.float32) * (4.0 / grid)
        square = z * z
        value = jnp.zeros_like(z)
        for k in (11, 9, 7, 5, 3, 1):
            term = (math.pi / 2) ** k / math.factorial(k) * (-1.0) ** (k // 2)
            value = value * square + term
        return value * -z

    def waves_of(shape):
        lane = lax.broadcasted_iota(jnp.int32, shape, 1)
        parity = (lane >= 2 * MAIN).astype(jnp.int32)
        column = lane - MAIN - parity * MAIN
        wave = jnp.where(
            lane < MAIN, lane + lax.axis_index("ga") * depth, 2 * column + parity
        )
        return wave, (lane < depth) | ((lane >= MAIN) & (column >= 0) & (wave < waves))

    def kernel(*refs):
        refs = list(refs)
        take = lambda count: [refs.pop(0) for _ in range(count)]
        (table_hbm,) = take(1)
        row_hbm = take(1)[0] if make_plane else None
        piece_hbm = take(n_piece)
        plane_in = take(len(plane))
        vec_refs = take(len(vecs))
        list_in = take(len(begun))[2:]
        vale_ref, cond_ref = take(2)
        (list_ref,) = list_in or take(1)
        vec_out = take(n_vec)
        plane_out = take(5 if make_plane else 0)
        table_ref, ket_raw, vplane, eplane, oplane = take(5)
        row_raw, cos_part, sin_part = take(3 if make_plane else 0) or (None,) * 3
        vec_raw = take(1)[0] if side else None
        bras, kets, fv, fe, fo, natural, vbuf, cbuf, seen = take(9)
        load_sem, out_sem, plane_sem = take(3)

        me = lax.axis_index("ka")
        source = me if side == 0 else mirror_of(me, ka_count)
        first = jnp.where(me < half, 0, half)

        loads = [pltpu.make_async_copy(table_hbm, table_ref, load_sem.at[0])]
        if make_plane:
            loads.append(pltpu.make_async_copy(row_hbm, row_raw, load_sem.at[1]))
        ready = len(loads)
        low = 0
        for i, ref in enumerate(piece_hbm):
            size = ref.shape[0]
            loads.append(
                pltpu.make_async_copy(
                    ref.at[:, pl.ds(0, grid)], ket_raw.at[pl.ds(low, size)], load_sem.at[2 + i]
                )
            )
            low += size
        for i, (ref, to) in enumerate(zip(plane_in, (vplane, eplane, oplane, bras, kets))):
            loads.append(pltpu.make_async_copy(ref, to, load_sem.at[4 + i]))
        if side:
            loads.append(
                pltpu.make_async_copy(
                    piece_hbm[0].at[:, pl.ds(grid, pairs)],
                    vec_raw,
                    load_sem.at[9],
                )
            )
            vec_refs = [vec_raw]
            vec_count = vec_rows // point_local
            orders = [[n * 16 + b for n in range(vec_count) for b in range(point_local)]]
        else:
            orders = [range(vec_rows)] * n_vec
        for load in loads:
            load.start()

        if make_plane:
            wave, valid = waves_of(cos_part.shape)
            point = lax.broadcasted_iota(jnp.int32, cos_part.shape, 0)
            scale = jnp.where(valid, math.sqrt(2.0 / grid), 0.0)
            cos_part[...] = cosine(wave * point) * scale
            sin_part[...] = cosine(wave * point - grid // 4) * scale
            wave8, _ = waves_of((8, cos_part.shape[1]))

            def fill(step, carry):
                at = pl.ds(pl.multiple_of(step * TAIL, TAIL), TAIL)
                turn = wave8 * (step * TAIL)
                value = cosine(turn)[:1] * cos_part[...]
                value -= cosine(turn - grid // 4)[:1] * sin_part[...]
                value = value.astype(jnp.bfloat16)
                vplane[at, :] = value[:, :depth]
                eplane[at, :] = value[:, MAIN : MAIN + evens]
                oplane[at, :] = value[:, 2 * MAIN : 2 * MAIN + odds]
                return carry

            def fill_back(step, carry):
                at = pl.ds(pl.multiple_of(segment + step * TAIL, TAIL), TAIL)
                turn = wave8[:, :MAIN] * (grid // 2 - step * TAIL)
                value = cosine(turn)[:1] * cos_part[:, :MAIN]
                value += cosine(turn - grid // 4)[:1] * sin_part[:, :MAIN]
                vplane[at, :] = value.astype(jnp.bfloat16)[:, :depth]
                return carry

            lax.fori_loop(0, segment // TAIL, fill, 0)
            lax.fori_loop(0, quarter // TAIL, fill_back, 0)

        at = lax.broadcasted_iota(jnp.int32, (2 * block, block), 0)
        to = lax.broadcasted_iota(jnp.int32, (2 * block, block), 1)
        flip = ((at < block) & (at + to == block)) | ((at == block) & (to == 0))
        flip = jnp.where(flip, 1.0, 0.0).astype(jnp.bfloat16)

        def fold(src, low, size, put):
            rows_at = slice(low, low + size)
            lane = lax.broadcasted_iota(jnp.int32, (size, block), 1)

            def turned(begin, end):
                return jnp.dot(
                    src[rows_at, begin:end], flip[: end - begin], preferred_element_type=jnp.float32
                )

            for at in range(0, quarter, block):
                end = grid - at - block
                there = src[rows_at, grid // 2 + at : grid // 2 + at + block].astype(jnp.float32)
                parts = (
                    src[rows_at, at : at + block].astype(jnp.float32),
                    turned(end, min(end + 2 * block, grid)),
                    turned(end - grid // 2, end - grid // 2 + 2 * block),
                    there if at else jnp.where(lane == 0, 0.0, there),
                )
                for k, values in enumerate(parts):
                    put(slice(k * segment + at, k * segment + at + block), values)
            for k in range(2):
                at = (2 * k + 1) * quarter
                last = src[rows_at, at : at + TAIL].astype(jnp.float32)
                at = k * segment + quarter
                put(slice(at, at + TAIL), jnp.where(lane[:, :TAIL] == 0, last, 0.0))

        def put_whole(ref):
            def put(lanes, values):
                ref[:, :, :, lanes] = values.reshape(-1, 2, 16, values.shape[1])

            return put

        def put_part(ref, kind):
            def put(lanes, values):
                for b in range(point_local):
                    ref[b, kind, :, lanes] = values[b * 16 : (b + 1) * 16]

            return put

        stores = []
        if make_plane:
            loads[1].wait()
            fold(row_raw, 0, row_raw.shape[0], put_whole(bras))
            stores = [
                pltpu.make_async_copy(ref, to, plane_sem.at[i])
                for i, (ref, to) in enumerate(zip((vplane, eplane, oplane, bras, kets), plane_out))
            ]
            for store in stores[:4]:
                store.start()
        for i in range(n_piece):
            loads[ready + i].wait()
        if n_piece == 1:
            fold(ket_raw, 0, ket_raw.shape[0], put_whole(kets))
            stores[4].start()
        elif n_piece:
            kind = lax.axis_index("ga") % 2
            size = point_local * 16
            fold(ket_raw, 0, size, put_part(kets, kind))
            fold(ket_raw, size, size, put_part(kets, 1 - kind))
        for load in loads[:1] + loads[ready + n_piece :]:
            load.wait()
        for i in range(n_vec):
            vec_out[i][...] = spread_vectors(vec_refs[i], i == 0, orders[i])

        def listed(p, carry):
            b = p // row_count
            a = lax.rem(p, row_count)
            owner = table_ref[a, source * point_local + b] // block_local - first

            @pl.when((owner >= 0) & (owner < half))
            def _():
                at = list_ref[0]
                list_ref[1 + 3 * at] = p
                list_ref[2 + 3 * at] = owner
                list_ref[3 + 3 * at] = seen[owner]
                list_ref[0] = at + 1
                seen[owner] = seen[owner] + 1

            return carry

        if not resume:
            for t in range(half):
                seen[t] = 0
            for f in range(4):
                list_ref[f] = 0
            lax.fori_loop(0, pair_count, listed, 0)
        count = list_ref[0]
        trips = (count + GROUP - 1) // GROUP
        begin = jnp.minimum(SPLIT, trips) if resume else 0
        end = jnp.minimum(SPLIT, trips) if make_plane else trips

        def outputs(n, g):
            slot = lax.rem(n, 2)
            p = list_ref[1 + 3 * jnp.minimum(n * GROUP + g, pair_count - 1)]
            return (
                pltpu.make_async_copy(vbuf.at[slot, g], vale_ref.at[p], out_sem.at[slot, g, 0]),
                pltpu.make_async_copy(cbuf.at[slot, g], cond_ref.at[p], out_sem.at[slot, g, 1]),
            )

        def finish(n):
            for g in range(GROUP):

                @pl.when((n >= begin) & (n * GROUP + g < count))
                def _():
                    for copy in outputs(n, g):
                        copy.wait()

        def group(n, carry):
            finish(n - 2)
            slot = lax.rem(n, 2)
            entries = [list_ref[1 + 3 * jnp.minimum(n * GROUP + g, count - 1)] for g in range(GROUP)]
            places = [(lax.rem(p, row_count), p // row_count) for p in entries]

            def products(kind, t):
                spans = range(4 if t < quarter else 2)
                lanes = [slice(k * segment + t, k * segment + t + 128) for k in spans]
                for g, (a, b) in enumerate(places):
                    ket = [kets[b, kind, :, at] for at in lanes]
                    for c in range(16):
                        bra = [bras[a, kind, c : c + 1, at] for at in lanes]
                        row = g * pairs + c * 16
                        yield slice(row, row + 16), [
                            bra[k] * ket[k] + bra[k + 1] * ket[k + 1] for k in spans[::2]
                        ]

            def times(lhs, low, high, plane_ref, total):
                part = jnp.dot(
                    lhs[:, low:high], plane_ref[low:high, :], preferred_element_type=jnp.float32
                )
                return part if total is None else total + part

            sums = {"vale": None, "even": None, "odd": None}

            def cond_products(low, high):
                for t in range(low, high, 128):
                    for at, value in products(1, t):
                        if t < quarter:
                            fe[at, t : t + 128] = (value[0] + value[1]).astype(jnp.bfloat16)
                            fo[at, t : t + 128] = (value[0] - value[1]).astype(jnp.bfloat16)
                        else:
                            fe[at, t : t + 128] = value[0].astype(jnp.bfloat16)

            def cond_sums(low, high):
                sums["even"] = times(fe, low, high, eplane, sums["even"])
                if low < quarter:
                    sums["odd"] = times(fo, low, high, oplane, sums["odd"])

            def vale_products(low, high):
                for t in range(low, high, 128):
                    for at, value in products(0, t):
                        for k, part in enumerate(value):
                            to = k * segment + t
                            fv[at, to : to + 128] = part.astype(jnp.bfloat16)

            def vale_sums(low, high):
                sums["vale"] = times(fv, low, high, vplane, sums["vale"])
                if low < quarter:
                    sums["vale"] = times(fv, segment + low, segment + high, vplane, sums["vale"])

            def cond_out():
                rest = waves - MAIN
                blank = jnp.zeros((HALF - rest, pairs), jnp.bfloat16)
                for g in range(GROUP):
                    for h in range(pairs // 128):
                        rows_at = slice(g * pairs + h * 128, g * pairs + (h + 1) * 128)
                        lanes = slice(h * 128, (h + 1) * 128)
                        natural[h, pl.ds(0, evens, stride=2), :] = sums["even"][rows_at].T
                        natural[h, pl.ds(1, odds, stride=2), :] = sums["odd"][rows_at].T
                        cbuf[slot, g, :waves, lanes] = natural[h, :waves].astype(jnp.bfloat16)
                        cbuf[slot, g, MAIN + HALF : waves + HALF, lanes] = natural[
                            h, MAIN:waves
                        ].astype(jnp.bfloat16)
                    cbuf[slot, g, waves : MAIN + HALF] = blank
                    cbuf[slot, g, waves + HALF :] = blank

            chunks = [(low, min(low + CHUNK, segment)) for low in range(0, segment, CHUNK)]
            steps = [(cond_products, cond_sums, chunk) for chunk in chunks]
            steps += [(vale_products, vale_sums, chunk) for chunk in chunks]
            steps[0][0](*steps[0][2])
            for at, (_, add, chunk) in enumerate(steps):
                if at + 1 < len(steps):
                    steps[at + 1][0](*steps[at + 1][2])
                add(*chunk)
                if at == len(chunks):
                    cond_out()
            vbuf[slot] = sums["vale"].astype(jnp.bfloat16).reshape(GROUP, pairs, depth)
            for g in range(GROUP):

                @pl.when(n * GROUP + g < count)
                def _():
                    for copy in outputs(n, g):
                        copy.start()

            return carry

        lax.fori_loop(begin, end, group, 0)
        finish(end - 2)
        finish(end - 1)
        for store in stores:
            store.wait()

    folded = lambda count: pltpu.VMEM((count, 2, 16, 4 * segment), jnp.float32)
    plane_shapes = [
        jax.ShapeDtypeStruct((points, depth), jnp.bfloat16),
        jax.ShapeDtypeStruct((segment, evens), jnp.bfloat16),
        jax.ShapeDtypeStruct((segment, odds), jnp.bfloat16),
        jax.ShapeDtypeStruct((row_count, 2, 16, 4 * segment), jnp.float32),
        jax.ShapeDtypeStruct((point_local, 2, 16, 4 * segment), jnp.float32),
    ]
    n_in = 1 + len(rows) + n_piece + len(plane)
    n_list = 0 if resume else 1
    result = pl.pallas_call(
        kernel,
        out_shape=[
            jax.ShapeDtypeStruct((pair_count, pairs, depth), jnp.bfloat16),
            jax.ShapeDtypeStruct((pair_count, width, pairs), jnp.bfloat16),
        ]
        + [jax.ShapeDtypeStruct((1 + 3 * pair_count,), jnp.int32)] * n_list
        + [jax.ShapeDtypeStruct((vec_rows, 16, pairs), jnp.float32)] * n_vec
        + (plane_shapes if make_plane else []),
        in_specs=[HBM] * n_in + [VMEM] * len(vecs) + ([HBM, HBM, SMEM] if resume else []),
        out_specs=[HBM, HBM]
        + [SMEM] * n_list
        + [VMEM] * n_vec
        + ([HBM] * len(plane_shapes) if make_plane else []),
        input_output_aliases={n_in: 0, n_in + 1: 1} if resume else {},
        scratch_shapes=[
            pltpu.SMEM(table.shape, jnp.int32),
            pltpu.VMEM((point_local * 32, grid), jnp.bfloat16),
            pltpu.VMEM((points, depth), jnp.bfloat16),
            pltpu.VMEM((segment, evens), jnp.bfloat16),
            pltpu.VMEM((segment, odds), jnp.bfloat16),
        ]
        + (
            [
                pltpu.VMEM(rows[0].shape, jnp.bfloat16),
                pltpu.VMEM((TAIL, 3 * MAIN), jnp.float32),
                pltpu.VMEM((TAIL, 3 * MAIN), jnp.float32),
            ]
            if make_plane
            else [pltpu.VMEM((point_local * 16, pairs), jnp.bfloat16)] * side
        )
        + [
            folded(row_count),
            folded(point_local),
            pltpu.VMEM((GROUP * pairs, points), jnp.bfloat16),
            pltpu.VMEM((GROUP * pairs, segment), jnp.bfloat16),
            pltpu.VMEM((GROUP * pairs, quarter), jnp.bfloat16),
            pltpu.VMEM((pairs // 128, 2 * evens, 128), jnp.float32),
            pltpu.VMEM((2, GROUP, pairs, depth), jnp.bfloat16),
            pltpu.VMEM((2, GROUP, width, pairs), jnp.bfloat16),
            pltpu.SMEM((half,), jnp.int32),
            pltpu.SemaphoreType.DMA((10,)),
            pltpu.SemaphoreType.DMA((2, GROUP, 2)),
            pltpu.SemaphoreType.DMA((5,)),
        ],
        compiler_params=pltpu.CompilerParams(vmem_limit_bytes=LIMIT if make_plane else WHOLE),
        cost_estimate=pl.CostEstimate(
            flops=5 * 10**10 if side else 1, bytes_accessed=10**6, transcendentals=0
        ),
        name="densities_mirror" if side else "densities_rest" if resume else "densities_own",
    )(table, *rows, *pieces, *plane, *vecs, *begun)
    if resume:
        return (*result, begun[2])
    return result[:3], result[3 : 3 + n_vec], result[3 + n_vec :]


def images(incoming, sides, vecs, row_vec, counts, row_scale, col_scale, wave_count):
    pair_count, pairs, depth = sides[0][0].shape
    width = sides[0][1].shape[1]
    vec_count, row_count, point_local = counts
    rest = wave_count - MAIN
    most = SIDES * pair_count

    def kernel(*refs):
        refs = list(refs)
        take = lambda count: [refs.pop(0) for _ in range(count)]
        (block_ref,) = take(1)
        side_refs = [take(3) for _ in range(SIDES)]
        vec_hbm = take(SIDES)
        rowvec_hbm, out_ref = take(2)
        block_buf, vale_buf, cond_buf, vec_buf, rowvec_ref, ready, even, odd, row_sum, col_sum = take(10)
        main_sem, shared_sem, vale_sem, cond_sem, vec_sem = take(5)

        own_count = side_refs[0][2][0]
        count = own_count + side_refs[1][2][0]

        def field(i, f):
            i = jnp.clip(i, 0, count - 1)
            own = side_refs[0][2][1 + 3 * jnp.minimum(i, pair_count - 1) + f]
            other = side_refs[1][2][1 + 3 * jnp.maximum(i - own_count, 0) + f]
            return jnp.where(i < own_count, own, other)

        def copies(k, i):
            vale_ref, cond_ref, _ = side_refs[k]
            p, owner, rank = (field(i, f) for f in range(3))
            lanes = pl.ds(pl.multiple_of(rank * MAIN, MAIN), MAIN)
            return (
                pltpu.make_async_copy(vale_ref.at[p], vale_buf.at[i], vale_sem.at[i]),
                pltpu.make_async_copy(
                    block_ref.at[owner, k, :, lanes],
                    block_buf.at[i, :, pl.ds(0, MAIN)],
                    main_sem.at[i],
                ),
                pltpu.make_async_copy(
                    block_ref.at[owner, k, :, pl.ds(CAP * MAIN, 2 * HALF)],
                    block_buf.at[i, :, pl.ds(MAIN, 2 * HALF)],
                    shared_sem.at[i],
                ),
                pltpu.make_async_copy(cond_ref.at[p], cond_buf.at[i], cond_sem.at[i]),
            )

        def start(i):
            for k in range(SIDES):
                low = own_count if k else 0
                high = count if k else own_count

                @pl.when((i >= low) & (i < high))
                def _():
                    for copy in copies(k, i):
                        copy.start()

        def arrived(i):
            for copy in copies(0, i):
                copy.wait()

        for i in range(AHEAD):
            start(i)
        vec_copies = [
            pltpu.make_async_copy(ref, to, vec_sem.at[k])
            for k, (ref, to) in enumerate(
                [(rowvec_hbm, rowvec_ref)] + [(vec_hbm[k], vec_buf.at[k]) for k in range(SIDES)]
            )
        ]
        for copy in vec_copies:
            copy.start()
        row_sum[...] = jnp.zeros(row_sum.shape, jnp.float32)
        col_sum[...] = jnp.zeros(col_sum.shape, jnp.float32)
        odd[...] = jnp.zeros(odd.shape, jnp.float32)
        for copy in vec_copies:
            copy.wait()

        def screen(i):
            at = jnp.minimum(i, count - 1)
            lane = lax.broadcasted_iota(jnp.int32, (depth, 2 * HALF), 1)
            begin = field(i, 2) * HALF
            mine = (lane >= begin) & (lane < begin + rest)
            shared = jnp.where(mine, block_buf[at, :, MAIN:].astype(jnp.float32), 0.0)
            block = jnp.concatenate([block_buf[at, :, :MAIN], shared.astype(jnp.bfloat16)], axis=1)
            return jnp.dot(block, cond_buf[at], preferred_element_type=jnp.float32).astype(
                jnp.bfloat16
            )

        def multiply(i, screened, into):
            at = jnp.minimum(i, count - 1)
            matrix = jnp.dot(vale_buf[at], screened, preferred_element_type=jnp.float32)
            into[...] = jnp.where(i < count, matrix, 0.0)

        def contract(i, matrix):
            p = field(i, 0)
            k = (jnp.clip(i, 0, count - 1) >= own_count).astype(jnp.int32)
            b = p // row_count
            a = lax.rem(p, row_count)
            totals = [jnp.zeros((16, pairs), jnp.float32)] * vec_count
            ket = [vec_buf[k, n * point_local + b] for n in range(vec_count)]
            for v in range(16):
                part = matrix[v * 16 : (v + 1) * 16, :]
                for n in range(vec_count):
                    term = part * ket[n]
                    row_sum[n, a, v] += term[:8] + term[8:]
                    totals[n] += part * rowvec_ref[n * row_count + a, v : v + 1, :]
            for n in range(vec_count):
                col_sum[k, n, b] += totals[n]

        def arrive(i):
            @pl.when(i < count)
            def _():
                arrived(i)

        @pl.when(count > 0)
        def _():
            for i in range(2):
                arrive(i)
            for i in range(2):
                ready[i] = screen(i)

        def two(j, carry):
            for i in range(2):
                start(2 * j + AHEAD + i)
            for i in range(2):
                arrive(2 * j + 2 + i)
            multiply(2 * j, ready[0], even)
            first = screen(2 * j + 2)
            contract(2 * j - 1, odd)
            multiply(2 * j + 1, ready[1], odd)
            second = screen(2 * j + 3)
            contract(2 * j, even)
            ready[0] = first
            ready[1] = second
            return carry

        trips = (count + 1) // 2
        lax.fori_loop(0, trips, two, 0)

        @pl.when(count > 0)
        def _():
            contract(2 * trips - 1, odd)

        def spread(values, keep_first, scale):
            at = lax.broadcasted_iota(jnp.int32, (pairs, pairs), 0)
            to = lax.broadcasted_iota(jnp.int32, (pairs, pairs), 1)
            index = at // 16 if keep_first else at % 16
            pick = jnp.where(index == to % 16, 1.0, 0.0).astype(jnp.bfloat16)
            high = values.astype(jnp.bfloat16)
            low = (values - high.astype(jnp.float32)).astype(jnp.bfloat16)
            wide = jnp.dot(high, pick, preferred_element_type=jnp.float32) + jnp.dot(
                low, pick, preferred_element_type=jnp.float32
            )
            row = lax.broadcasted_iota(jnp.int32, wide.shape, 0)
            lane = lax.broadcasted_iota(jnp.int32, wide.shape, 1)
            wide = jnp.where(row % 16 == lane // 16, wide, 0.0)
            return jnp.sum(wide.reshape(-1, 16, pairs), axis=1) * scale

        columns = spread(col_sum[...].reshape(-1, pairs), False, col_scale)
        summed = jnp.sum(row_sum[...].reshape(-1, 8, pairs), axis=1)
        summed = spread(summed, True, row_scale)
        for n in range(vec_count):
            out_ref[n] = columns[n * point_local : (n + 1) * point_local]
            out_ref[vec_count + n] = summed[n * row_count : (n + 1) * row_count]
            low = (vec_count + n) * point_local
            out_ref[2 * vec_count + n] = columns[low : low + point_local]

    assert point_local == row_count
    return pl.pallas_call(
        kernel,
        out_shape=jax.ShapeDtypeStruct((3 * vec_count, row_count, pairs), jnp.float32),
        in_specs=[HBM] + [HBM, HBM, SMEM] * SIDES + [HBM] * (SIDES + 1),
        out_specs=VMEM,
        scratch_shapes=[
            pltpu.VMEM((most, depth, WIDE_ONE), jnp.bfloat16),
            pltpu.VMEM((most, pairs, depth), jnp.bfloat16),
            pltpu.VMEM((most, width, pairs), jnp.bfloat16),
            pltpu.VMEM((SIDES,) + vecs[0].shape, jnp.float32),
            pltpu.VMEM(row_vec.shape, jnp.float32),
            pltpu.VMEM((2, depth, pairs), jnp.bfloat16),
            pltpu.VMEM((pairs, pairs), jnp.float32),
            pltpu.VMEM((pairs, pairs), jnp.float32),
            pltpu.VMEM((vec_count, row_count, 16, 8, pairs), jnp.float32),
            pltpu.VMEM((SIDES, vec_count, point_local, 16, pairs), jnp.float32),
        ]
        + [pltpu.SemaphoreType.DMA((most,))] * 4
        + [pltpu.SemaphoreType.DMA((SIDES + 1,))],
        compiler_params=pltpu.CompilerParams(vmem_limit_bytes=LIMIT),
        name="images",
    )(incoming, *sides[0], *sides[1], *vecs, row_vec)


def swap(values, axis, step):
    perm = [(i, i ^ step) for i in range(lax.axis_size(axis))]
    return lax.ppermute(values, axis, perm)


def on_device(row_orbitals, orbitals, screening, pair_blocks, row_vectors, vectors):
    ka_count = lax.axis_size("ka")
    ga_count = lax.axis_size("ga")
    half = ka_count // SIDES
    row_count = row_orbitals.shape[0]
    point_local, bands, grid = orbitals.shape
    block_local, wave_count, slice_width = screening.shape
    vec_count = vectors.shape[0]

    kind = lax.axis_index("ga") % 2
    part = lax.dynamic_slice_in_dim(orbitals, kind * NV, NV, 1)
    assert vec_count == point_local
    flat = lambda values: values.reshape(-1, NV * NC)
    beside = jnp.pad(vectors, ((0, 0), (0, NV - point_local), (0, 0)))
    part = jnp.concatenate([part, beside], axis=2).reshape(point_local * NV, -1)
    fetched = swap(part, "ka", half)

    table = pair_blocks.T
    outgoing = gather_blocks(table, jnp.swapaxes(screening, 1, 2), ka_count)
    outgoing, table = lax.optimization_barrier((outgoing, table))
    groups = [list(range(half)), list(range(half, ka_count))]
    incoming = lax.all_to_all(
        outgoing, "ka", split_axis=0, concat_axis=0, tiled=True, axis_index_groups=groups
    )

    rows = row_orbitals.reshape(row_count * bands, grid)
    sizes = (ka_count, block_local, slice_width, wave_count, vec_count * point_local, grid)
    own, (own_vec, row_vec), plane = densities(
        0,
        table,
        (rows,),
        (orbitals.reshape(point_local * bands, grid),),
        (),
        (flat(vectors), flat(row_vectors)),
        sizes,
    )
    fetched, own = lax.optimization_barrier((fetched, tuple(own)))
    passed = swap(fetched, "ga", 1)
    own = densities(0, table, (), (), plane, (), sizes, own)
    mirrored, (mirror_vec,), _ = densities(
        1, table, (), (fetched, passed), plane[:4], (), sizes
    )
    row_scale = float(wave_count * NV * NC * point_local * ka_count) ** (-0.5)
    col_scale = float(wave_count * NV * NC * row_count) ** (-0.5)
    part = images(
        incoming,
        (own, mirrored),
        (own_vec, mirror_vec),
        row_vec,
        (vec_count, row_count, point_local),
        row_scale,
        col_scale,
        wave_count,
    )
    step = 2
    while step < ga_count:
        part = part + swap(part, "ga", step)
        step *= 2
    total = ka_count * ga_count
    across = [(i, (i ^ 1 ^ half * ga_count)) for i in range(total)]
    beside = swap(part, "ga", 1)
    opposite = swap(part, "ka", half)
    corner = lax.ppermute(part, ("ka", "ga"), across)
    other = opposite[vec_count:] + corner[vec_count:]
    near = part + beside
    row = near[vec_count : 2 * vec_count] + other[:vec_count]
    near, other, row = lax.optimization_barrier((near, other, row))
    column = near[:vec_count] + other[vec_count:]
    step = 1
    while step < half:
        row = row + swap(row, "ka", step)
        step *= 2
    return row, column


def solution(mesh):
    return jax.shard_map(
        on_device,
        mesh=mesh,
        in_specs=(P(), P("ka", None, None), P("ka", None, "ga"), P(), P(), P(None, "ka", None)),
        out_specs=(P(), P(None, "ka", None)),
        check_vma=False,
    )
```
